256 devices in a mesh: rep: 16 (over y_hi, z), loop: 8 (over x, core), seq: 2 (over y_lo).
Axes of the slice: x: 4, y: 4 (y_hi: 2, y_lo: 2; y = y_hi * 2 + y_lo), z: 8, core: 2. Of those that a mesh axis runs over, the one named last changes fastest.
Arguments:
- patches: bfloat16 [512, 256, 1152], P(('rep', 'loop', 'seq')), may hold values from -6 to 6
- positions: int32 [2, 512, 256], P(None, ('rep', 'loop', 'seq')), may hold values from 0 to 127, as said below
- counts: int32 [512], P(('rep', 'loop', 'seq')), may hold values from 2 to 256, as said below
- probe: bfloat16 [1152], replicated
- w_keyval: bfloat16 [1152, 2304], replicated, may hold values from -0.1875 to 0.1875
- w_out: bfloat16 [1152, 1152], replicated, may hold values from -0.1875 to 0.1875
- texts: bfloat16 [512, 1152], P(('rep', 'loop'), 'seq'), may hold values from -0.1875 to 0.1875
Outputs:
- txt_grad: float32 [512, 1152], P(('rep', 'loop'), 'seq')
- wo_grad: float32 [1152, 1152], P(('rep', 'loop'), 'seq')
The draws below stay inside these ranges and needn't reach their ends.
Inputs may be any that keep to these rules, and one draw needn't show every extreme that they name: `counts`: each image's patches fill a grid of c columns (2 to 32) and r rows, row by row; its count is r * c. Images whose index is a multiple of 4 fill all 256 slots, and so do those whose index is 1 more than a multiple of 4. `positions`: for slot p below the image's count, the row is p // c and the column p % c of that image's c columns; beyond it both are 0.
All inputs are finite; a program needn't handle non-finite values.
Results may differ from the reference program's by a relative error of at most 0.012.
Values may be sent and summed in bfloat16 or wider, within the bound.
No kernel may reach another device: no remote copies, remote signals or barrier semaphores. Data moves between devices by JAX's collectives and lax.ppermute only.
A program may use at most 64 MiB of HBM per device.

```python
import math
import jax
import jax.numpy as jnp
from jax import lax

D = 1152
HEADS = 16
HEAD_DIM = 72
GRID = 16
PATCHES = 256
IMG_DEV = 2
IMAGES = 512
N_LOOP = 8
N_SEQ = 2


def grid_shape(key):
    cols = jax.random.randint(jax.random.fold_in(key, 11), (IMAGES,), 2, 2 * GRID + 1)
    cap = GRID * GRID // cols
    rows = jax.random.randint(jax.random.fold_in(key, 12), (IMAGES,), 0, 1 << 20) % cap + 1
    slot = jnp.arange(IMAGES, dtype=jnp.int32) % 4
    cols = jnp.where(slot == 0, GRID, jnp.where(slot == 1, 2, cols))
    rows = jnp.where(slot == 0, GRID, jnp.where(slot == 1, GRID * GRID // 2, rows))
    return (rows.astype(jnp.int32), cols.astype(jnp.int32))


def draw_counts(key, part):
    rows, cols = grid_shape(key)
    return (rows * cols).astype(jnp.int32)


def draw_positions(key, part):
    rows, cols = grid_shape(key)
    slots = jnp.arange(PATCHES, dtype=jnp.int32)[None, :]
    live = slots < (rows * cols)[:, None]
    row_pos = jnp.where(live, slots // cols[:, None], 0)
    col_pos = jnp.where(live, slots % cols[:, None], 0)
    return jnp.stack([row_pos, col_pos]).astype(jnp.int32)


def draw_probe(key, part):
    key = jax.random.fold_in(key, 5)
    values = jax.random.normal(key, (D,), jnp.float32)
    return values.astype(jnp.bfloat16)


def block_levels(stream_key, shape, pieces, least, high):
    level, own = 1.0, jax.random.fold_in(stream_key, 6)
    for position, parts in pieces:
        steps = jnp.exp(jax.random.uniform(jax.random.fold_in(own, position), (parts,), jnp.float32, least / len(pieces), high / len(pieces)))
        level = level * jnp.repeat(steps, shape[position] // parts).reshape([-1 if axis == position else 1 for axis in range(len(shape))])
    return level


def normal_values(rng, dims, scale, reach, cuts=(), kind=jnp.bfloat16):
    result = scale * jax.random.normal(rng, dims, jnp.float32)
    if cuts:
        result = result * block_levels(rng, dims, cuts, -0.22, 0.18)
    return jnp.clip(result, -reach, reach).astype(kind)


def setup_inputs(seed: int = 0) -> dict:
    splits = jax.random.split(jax.random.key(seed), 8)
    return {
        "patches": normal_values(splits[0], (IMAGES, PATCHES, D), 1.0, 6.0, ((0, 256),)),
        "positions": draw_positions(jax.random.fold_in(splits[7], 71), 0),
        "counts": draw_counts(jax.random.fold_in(splits[7], 71), 0),
        "probe": draw_probe(jax.random.fold_in(splits[7], 71), 0),
        "w_keyval": normal_values(splits[4], (D, 2 * D), D ** -0.5, 0.1875),
        "w_out": normal_values(splits[5], (D, D), D ** -0.5, 0.1875),
        "texts": normal_values(splits[6], (IMAGES, D), D ** -0.5, 0.1875, ((0, 128), (1, 2))),
    }


MASK_FILL = -1e+30
LOGIT_SCALE = 10.0
LOGIT_BIAS = -2.0

def rotate_keys(key_rows, row_pos, col_pos):
    count = key_rows.shape[0]
    quarter = HEAD_DIM // 4
    blocks = key_rows.reshape(count, HEADS, 2, 2, quarter)
    freqs = jnp.exp(jnp.arange(quarter, dtype=jnp.float32) * (-math.log(10000.0) / quarter))
    angles = jnp.stack([row_pos, col_pos], axis=1).astype(jnp.float32)[:, :, None] * freqs
    cosine = jnp.cos(angles)[:, None]
    sine = jnp.sin(angles)[:, None]
    first_half = blocks[:, :, :, 0]
    second_half = blocks[:, :, :, 1]
    turned = jnp.stack([first_half * cosine - second_half * sine, first_half * sine + second_half * cosine], axis=3)
    return turned.reshape(count, HEADS * HEAD_DIM)

def pool_block(patch_block, pos_block, count_block, probe, w_keyval):
    images = patch_block.shape[0]
    key_value = jnp.dot(patch_block.reshape(images * PATCHES, D), w_keyval, preferred_element_type=jnp.float32)
    key_rows = rotate_keys(key_value[:, :D], pos_block[0].reshape(-1), pos_block[1].reshape(-1))
    value_rows = key_value[:, D:].astype(jnp.bfloat16).reshape(images, PATCHES, HEADS, HEAD_DIM)
    scores = (key_rows * probe.astype(jnp.float32)).reshape(images, PATCHES, HEADS, HEAD_DIM).sum(axis=3) * HEAD_DIM ** (-0.5)
    live = (jnp.arange(PATCHES, dtype=jnp.int32)[None, :] < count_block[:, None])[:, :, None]
    scores = jnp.where(live, scores, MASK_FILL)
    top = scores.max(axis=1)
    raised = jnp.where(live, jnp.exp(scores - top[:, None]), 0.0)
    total = raised.sum(axis=1)
    weights = raised.astype(jnp.bfloat16)
    summed = jnp.einsum('bph,bphd->bhd', weights.astype(jnp.float32), value_rows.astype(jnp.float32))
    return (summed / total[:, :, None]).reshape(images, D).astype(jnp.bfloat16)

def reference(patches, positions, counts, probe, w_keyval, w_out, texts):
    blocks = IMAGES // IMG_DEV
    patch_blocks = patches.reshape(blocks, IMG_DEV, PATCHES, D)
    pos_blocks = positions.reshape(2, blocks, IMG_DEV, PATCHES).transpose(1, 0, 2, 3)
    count_blocks = counts.reshape(blocks, IMG_DEV)
    pooled = lax.map(lambda blocked: pool_block(blocked[0], blocked[1], blocked[2], probe, w_keyval), (patch_blocks, pos_blocks, count_blocks)).reshape(IMAGES, D)
    projected = jnp.dot(pooled, w_out, preferred_element_type=jnp.float32)
    length = jnp.sqrt(lax.optimization_barrier(jnp.sum(projected * projected, axis=1, keepdims=True)) + 1e-06)
    unit = projected / length
    embedded = unit.astype(jnp.bfloat16)
    group_rows = N_LOOP * N_SEQ * IMG_DEV
    groups = IMAGES // group_rows
    emb_groups = embedded.reshape(groups, group_rows, D).astype(jnp.float32)
    text_groups = texts.reshape(groups, group_rows, D).astype(jnp.float32)
    logit = LOGIT_SCALE * jnp.einsum('gid,gjd->gij', emb_groups, text_groups) + LOGIT_BIAS
    labels = 2.0 * jnp.eye(group_rows, dtype=jnp.float32) - 1.0
    pair_grad = (LOGIT_SCALE * (-labels * jax.nn.sigmoid(-labels * logit))).astype(jnp.bfloat16).astype(jnp.float32)
    image_grad = jnp.einsum('gij,gjd->gid', pair_grad, text_groups).reshape(IMAGES, D)
    txt_grad = jnp.einsum('gij,gid->gjd', pair_grad, emb_groups).reshape(IMAGES, D)
    inner = lax.optimization_barrier(jnp.sum(unit * image_grad, axis=1, keepdims=True))
    out_grad = ((image_grad - unit * inner) / length).astype(jnp.bfloat16)
    wo_grad = jnp.dot(pooled.T, out_grad, preferred_element_type=jnp.float32)
    return (txt_grad, wo_grad)
```

```python
import functools

import jax
import jax.numpy as jnp
import numpy as np
from jax import lax
from jax.experimental import pallas as pl
from jax.experimental.pallas import tpu as pltpu
from jax.sharding import PartitionSpec as P

WIDTH = 1152
HEADS = 16
HEAD_DIM = 72
HALF = HEAD_DIM // 2
QUARTER = HEAD_DIM // 4
SLOTS = 256
IMAGES = 2
POSITIONS = 128

MASK_FILL = -1e30
LOGIT_SCALE = 10.0
LOGIT_BIAS = -2.0

GROUP = 40
CHUNKS = ((0, 256), (256, 512), (512, 768), (768, 1024), (1024, 1152))
PAD_ROWS = 16

BF16 = jnp.bfloat16
F32 = jnp.float32


def angle_table():
    freqs = 10000.0 ** (-np.arange(QUARTER) / QUARTER)
    angles = np.arange(POSITIONS)[:, None] * freqs[None, :]
    table = np.zeros((2 * POSITIONS, 2 * POSITIONS), np.float32)
    for kind, value in enumerate((np.cos(angles), np.sin(angles))):
        high = value.astype(BF16).astype(np.float64)
        for part, entry in enumerate((high, value - high)):
            start = (2 * part + kind) * GROUP
            table[:POSITIONS, start : start + QUARTER] = entry
            table[POSITIONS:, start + QUARTER : start + HALF] = entry
    return table


def dot(left, right, left_axis=1, right_axis=0):
    return lax.dot_general(
        left, right, (((left_axis,), (right_axis,)), ((), ())), preferred_element_type=F32
    )


def split(value):
    high = value.astype(BF16)
    return high, (value - high.astype(F32)).astype(BF16)


def pool_kernel(
    counts, positions, probe, table, texts, patches_hbm, weights_hbm, out,
    patches, w_key, w_val, patch_sem, key_sem, val_sem,
):
    copies = []
    for image in range(IMAGES):
        copies.append(
            pltpu.make_async_copy(
                patches_hbm.at[image],
                patches.at[pl.ds(image * SLOTS, SLOTS)],
                patch_sem.at[image],
            )
        )
    key_copies = [
        pltpu.make_async_copy(
            weights_hbm.at[:, pl.ds(lo, hi - lo)], w_key.at[:, pl.ds(lo, hi - lo)], key_sem.at[n]
        )
        for n, (lo, hi) in enumerate(CHUNKS)
    ]
    val_copy = pltpu.make_async_copy(weights_hbm.at[:, pl.ds(WIDTH, WIDTH)], w_val, val_sem)
    copies[0].start()
    key_copies[0].start()
    copies[1].start()
    for copy in key_copies[1:]:
        copy.start()
    val_copy.start()

    pos = jnp.concatenate([positions[0], positions[1], jnp.zeros((4, SLOTS), jnp.int32)], axis=0)
    pos_t = jnp.transpose(pos.astype(F32))
    lane = lax.broadcasted_iota(jnp.int32, (SLOTS, POSITIONS), 1).astype(F32)
    hot = []
    for image in range(IMAGES):
        row = (pos_t[:, image : image + 1] == lane).astype(F32)
        col = (pos_t[:, 2 + image : 3 + image] == lane).astype(F32)
        hot.append(jnp.concatenate([row, col], axis=1))
    hot = jnp.concatenate(hot, axis=0).astype(BF16)
    cos_sin = dot(hot, table[...].astype(BF16)).astype(BF16)

    entry = lax.broadcasted_iota(jnp.int32, (8, WIDTH), 1) % HEAD_DIM
    within = entry % HALF
    own = jnp.broadcast_to(probe[...].astype(F32), (8, WIDTH))
    after = pltpu.roll(own, WIDTH - QUARTER, 1)
    before = pltpu.roll(own, QUARTER, 1)
    partner = jnp.where(within < QUARTER, after, -before)
    key = (entry // HALF) * QUARTER + within % QUARTER
    match = lax.broadcasted_iota(jnp.int32, (GROUP, WIDTH), 0) == key[:1]
    spread_cos = jnp.where(match, own[:1], 0.0)
    spread_sin = jnp.where(match, partner[:1], 0.0)
    spread = jnp.concatenate(
        [spread_cos, spread_sin, spread_cos, spread_sin,
         jnp.zeros((2 * POSITIONS - 4 * GROUP, WIDTH), F32)],
        axis=0,
    ).astype(BF16)

    head = lax.broadcasted_iota(jnp.int32, (HEADS, WIDTH), 0) * HEAD_DIM
    column = lax.broadcasted_iota(jnp.int32, (HEADS, WIDTH), 1)
    in_head = (column >= head) & (column < head + HEAD_DIM)
    head_rows = in_head.astype(F32).astype(BF16)

    copies[0].wait()
    copies[1].wait()
    scores = jnp.zeros((HEADS, IMAGES * SLOTS), F32)
    for n, (lo, hi) in enumerate(CHUNKS):
        key_copies[n].wait()
        keys = dot(patches[...], w_key[:, lo:hi])
        turned = keys * dot(cos_sin, spread[:, lo:hi])
        high, low = split(turned)
        rows = head_rows[:, lo:hi]
        scores += dot(rows, high, 1, 1) + dot(rows, low, 1, 1)
    scores *= HEAD_DIM ** (-0.5)

    slot = lax.broadcasted_iota(jnp.int32, (HEADS, SLOTS), 1)
    sums, totals = [], []
    for image in range(IMAGES):
        live = slot < counts[image]
        part = jnp.where(live, scores[:, image * SLOTS : (image + 1) * SLOTS], MASK_FILL)
        top = jnp.max(part, axis=1, keepdims=True)
        raised = jnp.where(live, jnp.exp(part - top), 0.0)
        totals.append(jnp.sum(raised, axis=1, keepdims=True))
        sums.append(dot(raised.astype(BF16), patches[pl.ds(image * SLOTS, SLOTS)]))
    high, low = split(jnp.concatenate(sums, axis=0))
    val_copy.wait()
    acc = dot(jnp.concatenate([high, low], axis=0), w_val[...])
    acc = acc[: IMAGES * HEADS] + acc[IMAGES * HEADS :]
    pooled = [
        jnp.sum(
            jnp.where(in_head, acc[image * HEADS : (image + 1) * HEADS] / totals[image], 0.0),
            axis=0,
            keepdims=True,
        )
        for image in range(IMAGES)
    ]
    text = texts[...].astype(F32)
    first = lax.axis_index("seq") == 0
    text = jnp.concatenate(
        [jnp.where(first, text, 0.0), jnp.where(first, 0.0, text)], axis=1
    )
    message = jnp.concatenate(pooled + [text, jnp.zeros((2, WIDTH), F32)], axis=0).astype(BF16)
    for peer in range(out.shape[0]):
        out[peer] = message


def pair_kernel(gathered, w_out, txt_grad, partial, pair_rows, pooled_rows):
    members = gathered.shape[0]
    images = IMAGES * members
    loops = members // 2
    own_rows = images // loops
    half = WIDTH // 2
    loop_index = lax.axis_index("loop")
    first = lax.axis_index("seq") == 0

    block = gathered[...].astype(F32).reshape(members * 8, WIDTH).astype(BF16)
    row = lax.broadcasted_iota(jnp.int32, (images, members * 8), 0)
    source = lax.broadcasted_iota(jnp.int32, (images, members * 8), 1)
    pick_image = source == (row // IMAGES) * 8 + row % IMAGES
    text_source = (row // own_rows) * 16 + 2 + row % own_rows
    pick_text = (source == text_source) | (source == text_source + 8)
    pick = jnp.concatenate([pick_image.astype(F32), pick_text.astype(F32)], axis=0).astype(BF16)
    compact = dot(pick, block)
    pooled_f32 = compact[:images]
    pooled = pooled_f32.astype(BF16)
    texts = compact[images:].astype(BF16)
    pooled_rows[:WIDTH] = jnp.transpose(pooled_f32)
    pooled_rows[WIDTH:] = jnp.zeros((pooled_rows.shape[0] - WIDTH, images), F32)

    projected = dot(pooled, w_out[...])
    length = jnp.sqrt(jnp.sum(projected * projected, axis=1, keepdims=True) + 1e-06)
    unit = projected / length
    embedded = unit.astype(BF16)
    logit = LOGIT_SCALE * dot(embedded, texts, 1, 1) + LOGIT_BIAS
    same = lax.broadcasted_iota(jnp.int32, (images, images), 0) == lax.broadcasted_iota(
        jnp.int32, (images, images), 1
    )
    labels = jnp.where(same, 1.0, -1.0)
    pair_grad = (LOGIT_SCALE * (-labels * jax.nn.sigmoid(-labels * logit))).astype(BF16)
    image_grad = dot(pair_grad, texts)
    inner = jnp.sum(unit * image_grad, axis=1, keepdims=True)
    out_grad = ((image_grad - unit * inner) / length).astype(F32)
    out_half = jnp.where(first, out_grad[:, :half], out_grad[:, half:]).astype(BF16)

    stride = loops * 9
    rows = jnp.concatenate(
        [
            pooled_rows[pl.ds(stride * rep + 9 * loop_index, PAD_ROWS), :]
            for rep in range(partial.shape[0])
        ],
        axis=0,
    ).astype(BF16)
    partial[...] = dot(rows, out_half).astype(BF16).reshape(partial.shape)

    pair_rows[:images] = jnp.transpose(pair_grad.astype(F32))
    pair_rows[images:] = jnp.zeros((pair_rows.shape[0] - images, images), F32)
    own = dot(pair_rows[pl.ds(own_rows * loop_index, 8), :].astype(BF16), embedded)
    txt_grad[...] = jnp.where(first, own[:own_rows, :half], own[:own_rows, half:])


def local(reps, members, patches, positions, counts, probe, w_keyval, w_out, texts):
    vmem = pl.BlockSpec(memory_space=pltpu.VMEM)
    smem = pl.BlockSpec(memory_space=pltpu.SMEM)
    hbm = pl.BlockSpec(memory_space=pltpu.HBM)
    message = pl.pallas_call(
        pool_kernel,
        name="pool",
        out_shape=jax.ShapeDtypeStruct((members, 8, WIDTH), BF16),
        in_specs=[smem, vmem, vmem, vmem, vmem, hbm, hbm],
        out_specs=vmem,
        scratch_shapes=[
            pltpu.VMEM((IMAGES * SLOTS, WIDTH), BF16),
            pltpu.VMEM((WIDTH, WIDTH), BF16),
            pltpu.VMEM((WIDTH, WIDTH), BF16),
            pltpu.SemaphoreType.DMA((IMAGES,)),
            pltpu.SemaphoreType.DMA((len(CHUNKS),)),
            pltpu.SemaphoreType.DMA,
        ],
        compiler_params=pltpu.CompilerParams(vmem_limit_bytes=40 * 1024 * 1024),
    )(counts, positions, probe.reshape(1, WIDTH), jnp.asarray(angle_table()), texts, patches, w_keyval)
    gathered = lax.all_to_all(message, ("loop", "seq"), split_axis=0, concat_axis=0, tiled=True)
    images = IMAGES * members
    txt_grad, partial = pl.pallas_call(
        pair_kernel,
        name="pairs",
        out_shape=(
            jax.ShapeDtypeStruct(texts.shape, F32),
            jax.ShapeDtypeStruct((reps, PAD_ROWS, WIDTH // 2), BF16),
        ),
        in_specs=[vmem, vmem],
        out_specs=(vmem, vmem),
        scratch_shapes=[
            pltpu.VMEM((images + 8, images), F32),
            pltpu.VMEM((WIDTH + 16, images), F32),
        ],
        compiler_params=pltpu.CompilerParams(vmem_limit_bytes=24 * 1024 * 1024),
    )(gathered, w_out)
    blocks = lax.all_to_all(partial, "rep", split_axis=0, concat_axis=0, tiled=True)
    wo_grad = jnp.sum(blocks.astype(F32), axis=0)[:9]
    return (txt_grad, wo_grad)


def solution(mesh):
    reps = mesh.shape["rep"]
    members = mesh.shape["loop"] * mesh.shape["seq"]
    return jax.shard_map(
        functools.partial(local, reps, members),
        mesh=mesh,
        in_specs=(
            P(("rep", "loop", "seq"), None, None),
            P(None, ("rep", "loop", "seq"), None),
            P(("rep", "loop", "seq")),
            P(),
            P(),
            P(),
            P(("rep", "loop"), "seq"),
        ),
        out_specs=(P(("rep", "loop"), "seq"), P(("rep", "loop"), "seq")),
        check_vma=False,
    )
```

```python
import functools

import jax
import jax.numpy as jnp
import numpy as np
from jax import lax
from jax.experimental import pallas as pl
from jax.experimental.pallas import tpu as pltpu
from jax.sharding import PartitionSpec as P

WIDTH = 1152
HEADS = 16
HEAD_DIM = 72
HALF = HEAD_DIM // 2
QUARTER = HEAD_DIM // 4
SLOTS = 256
IMAGES = 2
POSITIONS = 128

MASK_FILL = -1e30
LOGIT_SCALE = 10.0
LOGIT_BIAS = -2.0

GROUP = 40
PAD_ROWS = 16

BF16 = jnp.bfloat16
F32 = jnp.float32


def angle_table():
    freqs = 10000.0 ** (-np.arange(QUARTER) / QUARTER)
    angles = np.arange(POSITIONS)[:, None] * freqs[None, :]
    table = np.zeros((2 * POSITIONS, 2 * POSITIONS), np.float32)
    for kind, value in enumerate((np.cos(angles), np.sin(angles))):
        high = value.astype(BF16).astype(np.float64)
        for part, entry in enumerate((high, value - high)):
            start = (2 * part + kind) * GROUP
            table[:POSITIONS, start : start + QUARTER] = entry
            table[POSITIONS:, start + QUARTER : start + HALF] = entry
    return table


def dot(left, right, left_axis=1, right_axis=0):
    return lax.dot_general(
        left, right, (((left_axis,), (right_axis,)), ((), ())), preferred_element_type=F32
    )


def split(value):
    high = value.astype(BF16)
    return high, (value - high.astype(F32)).astype(BF16)


def pool_kernel(
    counts_hbm, positions_hbm, probe_hbm, table_hbm, texts_hbm, patches_hbm, weights_hbm, out,
    counts, positions, probe, table, texts, patches, w_key, w_val,
    small_sem, patch_sem, key_sem, val_sem,
):
    small = [
        pltpu.make_async_copy(source, target, small_sem.at[n])
        for n, (source, target) in enumerate(
            (
                (positions_hbm, positions),
                (table_hbm, table),
                (probe_hbm, probe),
                (texts_hbm, texts),
                (counts_hbm, counts),
            )
        )
    ]
    copies = [
        pltpu.make_async_copy(
            patches_hbm.at[image],
            patches.at[pl.ds(image * SLOTS, SLOTS)],
            patch_sem.at[image],
        )
        for image in range(IMAGES)
    ]
    copies.append(
        pltpu.make_async_copy(weights_hbm.at[:, pl.ds(0, WIDTH)], w_key, key_sem)
    )
    val_copy = pltpu.make_async_copy(weights_hbm.at[:, pl.ds(WIDTH, WIDTH)], w_val, val_sem)
    for copy in small + copies + [val_copy]:
        copy.start()
    for copy in small:
        copy.wait()

    pos = jnp.concatenate([positions[0], positions[1], jnp.zeros((4, SLOTS), jnp.int32)], axis=0)
    pos_t = jnp.transpose(pos.astype(F32))
    lane = lax.broadcasted_iota(jnp.int32, (SLOTS, POSITIONS), 1).astype(F32)
    hot = []
    for image in range(IMAGES):
        row = (pos_t[:, image : image + 1] == lane).astype(F32)
        col = (pos_t[:, 2 + image : 3 + image] == lane).astype(F32)
        hot.append(jnp.concatenate([row, col], axis=1))
    hot = jnp.concatenate(hot, axis=0).astype(BF16)
    cos_sin = dot(hot, table[...].astype(BF16)).astype(BF16)

    entry = lax.broadcasted_iota(jnp.int32, (8, WIDTH), 1) % HEAD_DIM
    within = entry % HALF
    own = jnp.broadcast_to(probe[...].astype(F32).reshape(1, WIDTH), (8, WIDTH))
    after = pltpu.roll(own, WIDTH - QUARTER, 1)
    before = pltpu.roll(own, QUARTER, 1)
    partner = jnp.where(within < QUARTER, after, -before)
    key = (entry // HALF) * QUARTER + within % QUARTER
    match = lax.broadcasted_iota(jnp.int32, (GROUP, WIDTH), 0) == key[:1]
    spread_cos = jnp.where(match, own[:1], 0.0)
    spread_sin = jnp.where(match, partner[:1], 0.0)
    spread = jnp.concatenate(
        [spread_cos, spread_sin, spread_cos, spread_sin,
         jnp.zeros((2 * POSITIONS - 4 * GROUP, WIDTH), F32)],
        axis=0,
    ).astype(BF16)

    head = lax.broadcasted_iota(jnp.int32, (HEADS, WIDTH), 0) * HEAD_DIM
    column = lax.broadcasted_iota(jnp.int32, (HEADS, WIDTH), 1)
    in_head = (column >= head) & (column < head + HEAD_DIM)

    head_row = lax.broadcasted_iota(jnp.int32, (WIDTH, HEADS), 0)
    head_lane = lax.broadcasted_iota(jnp.int32, (WIDTH, HEADS), 1) * HEAD_DIM
    head_cols = (head_row >= head_lane) & (head_row < head_lane + HEAD_DIM)
    head_cols = head_cols.astype(F32).astype(BF16)

    for copy in copies:
        copy.wait()
    keys = dot(patches[...], w_key[...])
    high, low = split(keys * dot(cos_sin, spread))
    scores = jnp.transpose(dot(high, head_cols) + dot(low, head_cols)) * HEAD_DIM ** (-0.5)

    slot = lax.broadcasted_iota(jnp.int32, (HEADS, SLOTS), 1)
    sums, totals = [], []
    for image in range(IMAGES):
        live = slot < counts[image]
        part = jnp.where(live, scores[:, image * SLOTS : (image + 1) * SLOTS], MASK_FILL)
        top = jnp.max(part, axis=1, keepdims=True)
        raised = jnp.where(live, jnp.exp(part - top), 0.0)
        totals.append(jnp.sum(raised, axis=1, keepdims=True))
        sums.append(dot(raised.astype(BF16), patches[pl.ds(image * SLOTS, SLOTS)]))
    high, low = split(jnp.concatenate(sums, axis=0))
    val_copy.wait()
    acc = dot(jnp.concatenate([high, low], axis=0), w_val[...])
    acc = acc[: IMAGES * HEADS] + acc[IMAGES * HEADS :]
    pooled = [
        jnp.sum(
            jnp.where(in_head, acc[image * HEADS : (image + 1) * HEADS] / totals[image], 0.0),
            axis=0,
            keepdims=True,
        )
        for image in range(IMAGES)
    ]
    text = texts[...].astype(F32)
    pairs = [
        jnp.concatenate([text[n : n + 1], text[n + 1 : n + 2]], axis=1)
        for n in range(0, texts.shape[0], 2)
    ]
    message = jnp.concatenate(pooled + pairs, axis=0).astype(BF16)
    for peer in range(out.shape[0]):
        out[peer] = message


def pair_kernel(gathered, w_out, txt_grad, partial, pair_rows, pooled_rows):
    members = gathered.shape[0]
    images = IMAGES * members
    loops = members // 2
    own_rows = images // loops
    half = WIDTH // 2
    loop_index = lax.axis_index("loop")
    first = lax.axis_index("seq") == 0

    height = gathered.shape[1]
    block = gathered[...].astype(F32).reshape(members * height, WIDTH).astype(BF16)
    row = lax.broadcasted_iota(jnp.int32, (images, members * height), 0)
    source = lax.broadcasted_iota(jnp.int32, (images, members * height), 1)
    pick_image = source == (row // IMAGES) * height + row % IMAGES
    text_source = (row // own_rows) * 2 * height + IMAGES + (row % own_rows) // 2
    pick = [pick_image, source == text_source, source == text_source + height]
    pick = jnp.concatenate([one.astype(F32) for one in pick], axis=0).astype(BF16)
    compact = dot(pick, block)
    pooled_f32 = compact[:images]
    pooled = pooled_f32.astype(BF16)
    even = lax.broadcasted_iota(jnp.int32, (images, half), 0) % 2 == 0
    halves = [
        jnp.where(even, part[:, :half], part[:, half:])
        for part in (compact[images : 2 * images], compact[2 * images :])
    ]
    texts = jnp.concatenate(halves, axis=1).astype(BF16)
    pooled_rows[:WIDTH] = jnp.transpose(pooled_f32)
    pooled_rows[WIDTH:] = jnp.zeros((pooled_rows.shape[0] - WIDTH, images), F32)

    projected = dot(pooled, w_out[...])
    length = jnp.sqrt(jnp.sum(projected * projected, axis=1, keepdims=True) + 1e-06)
    unit = projected / length
    embedded = unit.astype(BF16)
    logit = LOGIT_SCALE * dot(embedded, texts, 1, 1) + LOGIT_BIAS
    same = lax.broadcasted_iota(jnp.int32, (images, images), 0) == lax.broadcasted_iota(
        jnp.int32, (images, images), 1
    )
    labels = jnp.where(same, 1.0, -1.0)
    pair_grad = (LOGIT_SCALE * (-labels * jax.nn.sigmoid(-labels * logit))).astype(BF16)
    image_grad = dot(pair_grad, texts)
    inner = jnp.sum(unit * image_grad, axis=1, keepdims=True)
    out_grad = ((image_grad - unit * inner) / length).astype(F32)
    out_half = jnp.where(first, out_grad[:, :half], out_grad[:, half:]).astype(BF16)

    stride = loops * 9
    rows = jnp.concatenate(
        [
            pooled_rows[pl.ds(stride * rep + 9 * loop_index, PAD_ROWS), :]
            for rep in range(partial.shape[0])
        ],
        axis=0,
    ).astype(BF16)
    partial[...] = dot(rows, out_half).astype(BF16).reshape(partial.shape)

    pair_rows[:images] = jnp.transpose(pair_grad.astype(F32))
    pair_rows[images:] = jnp.zeros((pair_rows.shape[0] - images, images), F32)
    own = dot(pair_rows[pl.ds(own_rows * loop_index, 8), :].astype(BF16), embedded)
    txt_grad[...] = jnp.where(first, own[:own_rows, :half], own[:own_rows, half:])


def local(reps, members, patches, positions, counts, probe, w_keyval, w_out, texts):
    vmem = pl.BlockSpec(memory_space=pltpu.VMEM)
    hbm = pl.BlockSpec(memory_space=pltpu.HBM)
    message = pl.pallas_call(
        pool_kernel,
        name="pool",
        out_shape=pltpu.VMEM((members, IMAGES + texts.shape[0] // 2, WIDTH), BF16),
        in_specs=[hbm] * 7,
        out_specs=vmem,
        scratch_shapes=[
            pltpu.SMEM((IMAGES,), jnp.int32),
            pltpu.VMEM(positions.shape, jnp.int32),
            pltpu.VMEM(probe.shape, BF16),
            pltpu.VMEM((2 * POSITIONS, 2 * POSITIONS), F32),
            pltpu.VMEM(texts.shape, BF16),
            pltpu.VMEM((IMAGES * SLOTS, WIDTH), BF16),
            pltpu.VMEM((WIDTH, WIDTH), BF16),
            pltpu.VMEM((WIDTH, WIDTH), BF16),
            pltpu.SemaphoreType.DMA((5,)),
            pltpu.SemaphoreType.DMA((IMAGES,)),
            pltpu.SemaphoreType.DMA,
            pltpu.SemaphoreType.DMA,
        ],
        compiler_params=pltpu.CompilerParams(vmem_limit_bytes=60 * 1024 * 1024),
    )(counts, positions, probe, jnp.asarray(angle_table()), texts, patches, w_keyval)
    message, w_out = lax.optimization_barrier((message, w_out))
    gathered = lax.all_to_all(message, ("loop", "seq"), split_axis=0, concat_axis=0, tiled=True)
    images = IMAGES * members
    txt_grad, partial = pl.pallas_call(
        pair_kernel,
        name="pairs",
        out_shape=(
            jax.ShapeDtypeStruct(texts.shape, F32),
            jax.ShapeDtypeStruct((reps, PAD_ROWS, WIDTH // 2), BF16),
        ),
        in_specs=[vmem, vmem],
        out_specs=(vmem, vmem),
        scratch_shapes=[
            pltpu.VMEM((images + 8, images), F32),
            pltpu.VMEM((WIDTH + 16, images), F32),
        ],
        compiler_params=pltpu.CompilerParams(vmem_limit_bytes=24 * 1024 * 1024),
    )(gathered, w_out)
    blocks = lax.all_to_all(partial, "rep", split_axis=0, concat_axis=0, tiled=True)
    wo_grad = jnp.sum(blocks.astype(F32), axis=0)[:9]
    return (txt_grad, wo_grad)


def solution(mesh):
    reps = mesh.shape["rep"]
    members = mesh.shape["loop"] * mesh.shape["seq"]
    return jax.shard_map(
        functools.partial(local, reps, members),
        mesh=mesh,
        in_specs=(
            P(("rep", "loop", "seq"), None, None),
            P(None, ("rep", "loop", "seq"), None),
            P(("rep", "loop", "seq")),
            P(),
            P(),
            P(),
            P(("rep", "loop"), "seq"),
        ),
        out_specs=(P(("rep", "loop"), "seq"), P(("rep", "loop"), "seq")),
        check_vma=False,
    )
```

```python
import functools

import jax
import jax.numpy as jnp
import numpy as np
from jax import lax
from jax.experimental import pallas as pl
from jax.experimental.pallas import tpu as pltpu
from jax.sharding import PartitionSpec as P

WIDTH = 1152
HEADS = 16
HEAD_DIM = 72
HALF = HEAD_DIM // 2
QUARTER = HEAD_DIM // 4
SLOTS = 256
IMAGES = 2
POSITIONS = 128

MASK_FILL = -1e30
LOGIT_SCALE = 10.0
LOGIT_BIAS = -2.0

GROUP = 40
OWN_ROWS = 9
FOLD = 8
FOLD_AT = 640
MESSAGE = 768

BF16 = jnp.bfloat16
F32 = jnp.float32


def angle_table():
    freqs = 10000.0 ** (-np.arange(QUARTER) / QUARTER)
    angles = np.arange(POSITIONS)[:, None] * freqs[None, :]
    table = np.zeros((2 * POSITIONS, 2 * POSITIONS), np.float32)
    for kind, value in enumerate((np.cos(angles), np.sin(angles))):
        high = value.astype(BF16).astype(np.float64)
        for part, entry in enumerate((high, value - high)):
            start = (2 * part + kind) * GROUP
            table[:POSITIONS, start : start + QUARTER] = entry
            table[POSITIONS:, start + QUARTER : start + HALF] = entry
    return table


def dot(left, right, left_axis=1, right_axis=0):
    return lax.dot_general(
        left, right, (((left_axis,), (right_axis,)), ((), ())), preferred_element_type=F32
    )


def split(value):
    high = value.astype(BF16)
    return high, (value - high.astype(F32)).astype(BF16)


def pool_kernel(
    counts_hbm, positions_hbm, probe_hbm, table_hbm, texts_hbm, patches_hbm, weights_hbm, out,
    counts, positions, probe, table, texts, patches, w_key, w_val,
    small_sem, patch_sem, key_sem, val_sem,
):
    small = [
        pltpu.make_async_copy(source, target, small_sem.at[n])
        for n, (source, target) in enumerate(
            (
                (positions_hbm, positions),
                (table_hbm, table),
                (probe_hbm, probe),
                (texts_hbm, texts),
                (counts_hbm, counts),
            )
        )
    ]
    copies = [
        pltpu.make_async_copy(
            patches_hbm.at[image],
            patches.at[pl.ds(image * SLOTS, SLOTS)],
            patch_sem.at[image],
        )
        for image in range(IMAGES)
    ]
    copies.append(
        pltpu.make_async_copy(weights_hbm.at[:, pl.ds(0, WIDTH)], w_key, key_sem)
    )
    val_copy = pltpu.make_async_copy(weights_hbm.at[:, pl.ds(WIDTH, WIDTH)], w_val, val_sem)
    for copy in small + copies + [val_copy]:
        copy.start()
    for copy in small:
        copy.wait()

    pos = jnp.concatenate([positions[0], positions[1], jnp.zeros((4, SLOTS), jnp.int32)], axis=0)
    pos_t = jnp.transpose(pos.astype(F32))
    lane = lax.broadcasted_iota(jnp.int32, (SLOTS, POSITIONS), 1).astype(F32)
    hot = []
    for image in range(IMAGES):
        row = (pos_t[:, image : image + 1] == lane).astype(F32)
        col = (pos_t[:, 2 + image : 3 + image] == lane).astype(F32)
        hot.append(jnp.concatenate([row, col], axis=1))
    hot = jnp.concatenate(hot, axis=0).astype(BF16)
    cos_sin = dot(hot, table[...].astype(BF16)).astype(BF16)

    entry = lax.broadcasted_iota(jnp.int32, (8, WIDTH), 1) % HEAD_DIM
    within = entry % HALF
    own = jnp.broadcast_to(probe[...].astype(F32).reshape(1, WIDTH), (8, WIDTH))
    after = pltpu.roll(own, WIDTH - QUARTER, 1)
    before = pltpu.roll(own, QUARTER, 1)
    partner = jnp.where(within < QUARTER, after, -before)
    key = (entry // HALF) * QUARTER + within % QUARTER
    match = lax.broadcasted_iota(jnp.int32, (GROUP, WIDTH), 0) == key[:1]
    spread_cos = jnp.where(match, own[:1], 0.0)
    spread_sin = jnp.where(match, partner[:1], 0.0)
    spread = jnp.concatenate(
        [spread_cos, spread_sin, spread_cos, spread_sin,
         jnp.zeros((2 * POSITIONS - 4 * GROUP, WIDTH), F32)],
        axis=0,
    ).astype(BF16)

    head = lax.broadcasted_iota(jnp.int32, (HEADS, WIDTH), 0) * HEAD_DIM
    column = lax.broadcasted_iota(jnp.int32, (HEADS, WIDTH), 1)
    in_head = (column >= head) & (column < head + HEAD_DIM)

    head_row = lax.broadcasted_iota(jnp.int32, (WIDTH, HEADS), 0)
    head_lane = lax.broadcasted_iota(jnp.int32, (WIDTH, HEADS), 1) * HEAD_DIM
    head_cols = (head_row >= head_lane) & (head_row < head_lane + HEAD_DIM)
    head_cols = head_cols.astype(F32).astype(BF16)

    for copy in copies:
        copy.wait()
    keys = dot(patches[...], w_key[...])
    high, low = split(keys * dot(cos_sin, spread))
    scores = jnp.transpose(dot(high, head_cols) + dot(low, head_cols)) * HEAD_DIM ** (-0.5)

    slot = lax.broadcasted_iota(jnp.int32, (HEADS, SLOTS), 1)
    sums, totals = [], []
    for image in range(IMAGES):
        live = slot < counts[image]
        part = jnp.where(live, scores[:, image * SLOTS : (image + 1) * SLOTS], MASK_FILL)
        top = jnp.max(part, axis=1, keepdims=True)
        raised = jnp.where(live, jnp.exp(part - top), 0.0)
        totals.append(jnp.sum(raised, axis=1, keepdims=True))
        sums.append(dot(raised.astype(BF16), patches[pl.ds(image * SLOTS, SLOTS)]))
    high, low = split(jnp.concatenate(sums, axis=0))
    val_copy.wait()
    acc = dot(jnp.concatenate([high, low], axis=0), w_val[...])
    acc = acc[: IMAGES * HEADS] + acc[IMAGES * HEADS :]
    pooled = [
        jnp.sum(
            jnp.where(in_head, acc[image * HEADS : (image + 1) * HEADS] / totals[image], 0.0),
            axis=0,
            keepdims=True,
        )
        for image in range(IMAGES)
    ]
    text = texts[...].astype(F32)
    pairs = [
        jnp.concatenate([text[n : n + 1], text[n + 1 : n + 2]], axis=1)
        for n in range(0, texts.shape[0], 2)
    ]
    message = jnp.concatenate(pooled + pairs, axis=0).astype(BF16)
    for peer in range(out.shape[0]):
        out[peer] = message


def pair_kernel(gathered, w_out, txt_grad, partial, pair_rows, pooled_rows, folded):
    members = gathered.shape[0]
    images = IMAGES * members
    loops = members // 2
    own_rows = images // loops
    half = WIDTH // 2
    loop_index = lax.axis_index("loop")
    first = lax.axis_index("seq") == 0

    height = gathered.shape[1]
    block = gathered[...].astype(F32).reshape(members * height, WIDTH).astype(BF16)
    row = lax.broadcasted_iota(jnp.int32, (images, members * height), 0)
    source = lax.broadcasted_iota(jnp.int32, (images, members * height), 1)
    pick_image = source == (row // IMAGES) * height + row % IMAGES
    text_source = (row // own_rows) * 2 * height + IMAGES + (row % own_rows) // 2
    pick = [pick_image, source == text_source, source == text_source + height]
    pick = jnp.concatenate([one.astype(F32) for one in pick], axis=0).astype(BF16)
    compact = dot(pick, block)
    pooled_f32 = compact[:images]
    pooled = pooled_f32.astype(BF16)
    even = lax.broadcasted_iota(jnp.int32, (images, half), 0) % 2 == 0
    halves = [
        jnp.where(even, part[:, :half], part[:, half:])
        for part in (compact[images : 2 * images], compact[2 * images :])
    ]
    texts = jnp.concatenate(halves, axis=1).astype(BF16)
    pooled_rows[:WIDTH] = jnp.transpose(pooled_f32)
    pooled_rows[WIDTH:] = jnp.zeros((pooled_rows.shape[0] - WIDTH, images), F32)

    projected = dot(pooled, w_out[...])
    length = jnp.sqrt(jnp.sum(projected * projected, axis=1, keepdims=True) + 1e-06)
    unit = projected / length
    embedded = unit.astype(BF16)
    logit = LOGIT_SCALE * dot(embedded, texts, 1, 1) + LOGIT_BIAS
    same = lax.broadcasted_iota(jnp.int32, (images, images), 0) == lax.broadcasted_iota(
        jnp.int32, (images, images), 1
    )
    labels = jnp.where(same, 1.0, -1.0)
    pair_grad = (LOGIT_SCALE * (-labels * jax.nn.sigmoid(-labels * logit))).astype(BF16)
    image_grad = dot(pair_grad, texts)
    inner = jnp.sum(unit * image_grad, axis=1, keepdims=True)
    out_grad = ((image_grad - unit * inner) / length).astype(F32)
    out_half = jnp.where(first, out_grad[:, :half], out_grad[:, half:]).astype(BF16)

    reps = partial.shape[0]
    stride = loops * OWN_ROWS
    start = OWN_ROWS * loop_index
    rows = jnp.concatenate(
        [pooled_rows[pl.ds(stride * rep + start, FOLD), :] for rep in range(reps)]
        + [pooled_rows[pl.ds(stride * rep + start + FOLD, 1), :] for rep in range(reps)],
        axis=0,
    ).astype(BF16)
    padded = jnp.concatenate([out_half, jnp.zeros((images, FOLD_AT - half), BF16)], axis=1)
    sums = dot(rows, padded)
    partial[:, :, :FOLD_AT] = sums[: reps * FOLD].reshape(reps, FOLD, FOLD_AT).astype(BF16)
    width = half // FOLD
    folded[...] = jnp.zeros(folded.shape, F32)
    for n in range(FOLD):
        folded[pl.ds(n, reps, FOLD), :width] = sums[reps * FOLD :, n * width : (n + 1) * width]
    partial[:, :, FOLD_AT:] = folded[...].reshape(reps, FOLD, MESSAGE - FOLD_AT).astype(BF16)

    pair_rows[:images] = jnp.transpose(pair_grad.astype(F32))
    pair_rows[images:] = jnp.zeros((pair_rows.shape[0] - images, images), F32)
    own = dot(pair_rows[pl.ds(own_rows * loop_index, 8), :].astype(BF16), embedded)
    txt_grad[...] = jnp.where(first, own[:own_rows, :half], own[:own_rows, half:])


def sum_kernel(blocks, out):
    total = jnp.sum(blocks[...].astype(F32), axis=0)
    half = out.shape[1]
    width = half // FOLD
    out[:FOLD] = total[:, :half]
    out[FOLD:] = jnp.concatenate(
        [total[n : n + 1, FOLD_AT : FOLD_AT + width] for n in range(FOLD)], axis=1
    )


def local(reps, members, patches, positions, counts, probe, w_keyval, w_out, texts):
    vmem = pl.BlockSpec(memory_space=pltpu.VMEM)
    hbm = pl.BlockSpec(memory_space=pltpu.HBM)
    message = pl.pallas_call(
        pool_kernel,
        name="pool",
        out_shape=pltpu.VMEM((members, IMAGES + texts.shape[0] // 2, WIDTH), BF16),
        in_specs=[hbm] * 7,
        out_specs=vmem,
        scratch_shapes=[
            pltpu.SMEM((IMAGES,), jnp.int32),
            pltpu.VMEM(positions.shape, jnp.int32),
            pltpu.VMEM(probe.shape, BF16),
            pltpu.VMEM((2 * POSITIONS, 2 * POSITIONS), F32),
            pltpu.VMEM(texts.shape, BF16),
            pltpu.VMEM((IMAGES * SLOTS, WIDTH), BF16),
            pltpu.VMEM((WIDTH, WIDTH), BF16),
            pltpu.VMEM((WIDTH, WIDTH), BF16),
            pltpu.SemaphoreType.DMA((5,)),
            pltpu.SemaphoreType.DMA((IMAGES,)),
            pltpu.SemaphoreType.DMA,
            pltpu.SemaphoreType.DMA,
        ],
        compiler_params=pltpu.CompilerParams(vmem_limit_bytes=60 * 1024 * 1024),
    )(counts, positions, probe, jnp.asarray(angle_table()), texts, patches, w_keyval)
    message, w_out = lax.optimization_barrier((message, w_out))
    gathered = lax.all_to_all(message, ("loop", "seq"), split_axis=0, concat_axis=0, tiled=True)
    images = IMAGES * members
    txt_grad, partial = pl.pallas_call(
        pair_kernel,
        name="pairs",
        out_shape=(
            jax.ShapeDtypeStruct(texts.shape, F32),
            jax.ShapeDtypeStruct((reps, FOLD, MESSAGE), BF16),
        ),
        in_specs=[vmem, vmem],
        out_specs=(vmem, vmem),
        scratch_shapes=[
            pltpu.VMEM((images + 8, images), F32),
            pltpu.VMEM((WIDTH + 16, images), F32),
            pltpu.VMEM((reps * FOLD, MESSAGE - FOLD_AT), F32),
        ],
        compiler_params=pltpu.CompilerParams(vmem_limit_bytes=24 * 1024 * 1024),
    )(gathered, w_out)
    blocks = lax.all_to_all(partial, "rep", split_axis=0, concat_axis=0, tiled=True)
    wo_grad = pl.pallas_call(
        sum_kernel,
        name="sums",
        out_shape=jax.ShapeDtypeStruct((OWN_ROWS, WIDTH // 2), F32),
        in_specs=[vmem],
        out_specs=vmem,
    )(blocks)
    return (txt_grad, wo_grad)


def solution(mesh):
    reps = mesh.shape["rep"]
    members = mesh.shape["loop"] * mesh.shape["seq"]
    return jax.shard_map(
        functools.partial(local, reps, members),
        mesh=mesh,
        in_specs=(
            P(("rep", "loop", "seq"), None, None),
            P(None, ("rep", "loop", "seq"), None),
            P(("rep", "loop", "seq")),
            P(),
            P(),
            P(),
            P(("rep", "loop"), "seq"),
        ),
        out_specs=(P(("rep", "loop"), "seq"), P(("rep", "loop"), "seq")),
        check_vma=False,
    )
```

```python
import functools

import jax
import jax.numpy as jnp
import numpy as np
from jax import lax
from jax.experimental import pallas as pl
from jax.experimental.pallas import tpu as pltpu
from jax.sharding import PartitionSpec as P

WIDTH = 1152
HEADS = 16
HEAD_DIM = 72
HALF = HEAD_DIM // 2
QUARTER = HEAD_DIM // 4
SLOTS = 256
IMAGES = 2
POSITIONS = 128

MASK_FILL = -1e30
LOGIT_SCALE = 10.0
LOGIT_BIAS = -2.0

GROUP = 40
OWN_ROWS = 9
FOLD = 8
FOLD_AT = 640
MESSAGE = 768

BF16 = jnp.bfloat16
F32 = jnp.float32


def angle_table():
    freqs = 10000.0 ** (-np.arange(QUARTER) / QUARTER)
    angles = np.arange(POSITIONS)[:, None] * freqs[None, :]
    table = np.zeros((2 * POSITIONS, 2 * POSITIONS), np.float32)
    for kind, value in enumerate((np.cos(angles), np.sin(angles))):
        high = value.astype(BF16).astype(np.float64)
        for part, entry in enumerate((high, value - high)):
            start = (2 * part + kind) * GROUP
            table[:POSITIONS, start : start + QUARTER] = entry
            table[POSITIONS:, start + QUARTER : start + HALF] = entry
    return table


def dot(left, right, left_axis=1, right_axis=0):
    return lax.dot_general(
        left, right, (((left_axis,), (right_axis,)), ((), ())), preferred_element_type=F32
    )


def split(value):
    high = value.astype(BF16)
    return high, (value - high.astype(F32)).astype(BF16)


def pool_kernel(
    counts_hbm, positions_hbm, probe_hbm, table_hbm, texts_hbm, patches_hbm, weights_hbm, out,
    counts, positions, probe, table, texts, patches, w_key, w_val,
    small_sem, patch_sem, key_sem, val_sem,
):
    small = [
        pltpu.make_async_copy(source, target, small_sem.at[n])
        for n, (source, target) in enumerate(
            (
                (positions_hbm, positions),
                (table_hbm, table),
                (probe_hbm, probe),
                (texts_hbm, texts),
                (counts_hbm, counts),
            )
        )
    ]
    copies = [
        pltpu.make_async_copy(
            patches_hbm.at[image],
            patches.at[pl.ds(image * SLOTS, SLOTS)],
            patch_sem.at[image],
        )
        for image in range(IMAGES)
    ]
    copies.append(
        pltpu.make_async_copy(weights_hbm.at[:, pl.ds(0, WIDTH)], w_key, key_sem)
    )
    val_copy = pltpu.make_async_copy(weights_hbm.at[:, pl.ds(WIDTH, WIDTH)], w_val, val_sem)
    for copy in small + copies + [val_copy]:
        copy.start()
    for copy in small:
        copy.wait()

    pos = jnp.concatenate([positions[0], positions[1], jnp.zeros((4, SLOTS), jnp.int32)], axis=0)
    pos_t = jnp.transpose(pos.astype(F32))
    lane = lax.broadcasted_iota(jnp.int32, (SLOTS, POSITIONS), 1).astype(F32)
    hot = []
    for image in range(IMAGES):
        row = (pos_t[:, image : image + 1] == lane).astype(F32)
        col = (pos_t[:, 2 + image : 3 + image] == lane).astype(F32)
        hot.append(jnp.concatenate([row, col], axis=1))
    hot = jnp.concatenate(hot, axis=0).astype(BF16)
    cos_sin = dot(hot, table[...].astype(BF16)).astype(BF16)

    entry = lax.broadcasted_iota(jnp.int32, (8, WIDTH), 1) % HEAD_DIM
    within = entry % HALF
    own = jnp.broadcast_to(probe[...].astype(F32).reshape(1, WIDTH), (8, WIDTH))
    after = pltpu.roll(own, WIDTH - QUARTER, 1)
    before = pltpu.roll(own, QUARTER, 1)
    partner = jnp.where(within < QUARTER, after, -before)
    key = (entry // HALF) * QUARTER + within % QUARTER
    match = lax.broadcasted_iota(jnp.int32, (GROUP, WIDTH), 0) == key[:1]
    spread_cos = jnp.where(match, own[:1], 0.0)
    spread_sin = jnp.where(match, partner[:1], 0.0)
    spread = jnp.concatenate(
        [spread_cos, spread_sin, spread_cos, spread_sin,
         jnp.zeros((2 * POSITIONS - 4 * GROUP, WIDTH), F32)],
        axis=0,
    ).astype(BF16)

    head = lax.broadcasted_iota(jnp.int32, (HEADS, WIDTH), 0) * HEAD_DIM
    column = lax.broadcasted_iota(jnp.int32, (HEADS, WIDTH), 1)
    in_head = (column >= head) & (column < head + HEAD_DIM)

    head_row = lax.broadcasted_iota(jnp.int32, (WIDTH, HEADS), 0)
    head_lane = lax.broadcasted_iota(jnp.int32, (WIDTH, HEADS), 1) * HEAD_DIM
    head_cols = (head_row >= head_lane) & (head_row < head_lane + HEAD_DIM)
    head_cols = head_cols.astype(F32).astype(BF16)

    for copy in copies:
        copy.wait()
    keys = dot(patches[...], w_key[...])
    high, low = split(keys * dot(cos_sin, spread))
    scores = jnp.transpose(dot(high, head_cols) + dot(low, head_cols)) * HEAD_DIM ** (-0.5)

    slot = lax.broadcasted_iota(jnp.int32, (HEADS, SLOTS), 1)
    sums, totals = [], []
    for image in range(IMAGES):
        live = slot < counts[image]
        part = jnp.where(live, scores[:, image * SLOTS : (image + 1) * SLOTS], MASK_FILL)
        top = jnp.max(part, axis=1, keepdims=True)
        raised = jnp.where(live, jnp.exp(part - top), 0.0)
        totals.append(jnp.sum(raised, axis=1, keepdims=True))
        sums.append(dot(raised.astype(BF16), patches[pl.ds(image * SLOTS, SLOTS)]))
    high, low = split(jnp.concatenate(sums, axis=0))
    val_copy.wait()
    acc = dot(jnp.concatenate([high, low], axis=0), w_val[...])
    acc = acc[: IMAGES * HEADS] + acc[IMAGES * HEADS :]
    pooled = [
        jnp.sum(
            jnp.where(in_head, acc[image * HEADS : (image + 1) * HEADS] / totals[image], 0.0),
            axis=0,
            keepdims=True,
        )
        for image in range(IMAGES)
    ]
    text = texts[...].astype(F32)
    pairs = [
        jnp.concatenate([text[n : n + 1], text[n + 1 : n + 2]], axis=1)
        for n in range(0, texts.shape[0], 2)
    ]
    message = jnp.concatenate(pooled + pairs, axis=0).astype(BF16)
    for peer in range(out.shape[0]):
        out[peer] = message


def pair_kernel(gathered, w_out, txt_grad, partial, pair_rows, pooled_rows, folded):
    members = gathered.shape[0]
    images = IMAGES * members
    loops = members // 2
    own_rows = images // loops
    half = WIDTH // 2
    loop_index = lax.axis_index("loop")
    first = lax.axis_index("seq") == 0

    height = gathered.shape[1]
    block = gathered[...].astype(F32).reshape(members * height, WIDTH).astype(BF16)
    row = lax.broadcasted_iota(jnp.int32, (images, members * height), 0)
    source = lax.broadcasted_iota(jnp.int32, (images, members * height), 1)
    pick_image = source == (row // IMAGES) * height + row % IMAGES
    text_source = (row // own_rows) * 2 * height + IMAGES + (row % own_rows) // 2
    pick = [pick_image, source == text_source, source == text_source + height]
    pick = jnp.concatenate([one.astype(F32) for one in pick], axis=0).astype(BF16)
    compact = dot(pick, block)
    pooled_f32 = compact[:images]
    pooled = pooled_f32.astype(BF16)
    even = lax.broadcasted_iota(jnp.int32, (images, half), 0) % 2 == 0
    halves = [
        jnp.where(even, part[:, :half], part[:, half:])
        for part in (compact[images : 2 * images], compact[2 * images :])
    ]
    texts = jnp.concatenate(halves, axis=1).astype(BF16)
    pooled_rows[:WIDTH] = jnp.transpose(pooled_f32)
    pooled_rows[WIDTH:] = jnp.zeros((pooled_rows.shape[0] - WIDTH, images), F32)

    projected = dot(pooled, w_out[...])
    length = jnp.sqrt(jnp.sum(projected * projected, axis=1, keepdims=True) + 1e-06)
    unit = projected / length
    embedded = unit.astype(BF16)
    logit = LOGIT_SCALE * dot(embedded, texts, 1, 1) + LOGIT_BIAS
    same = lax.broadcasted_iota(jnp.int32, (images, images), 0) == lax.broadcasted_iota(
        jnp.int32, (images, images), 1
    )
    labels = jnp.where(same, 1.0, -1.0)
    pair_grad = (LOGIT_SCALE * (-labels * jax.nn.sigmoid(-labels * logit))).astype(BF16)
    image_grad = dot(pair_grad, texts)
    inner = jnp.sum(unit * image_grad, axis=1, keepdims=True)
    out_grad = ((image_grad - unit * inner) / length).astype(F32)
    out_half = jnp.where(first, out_grad[:, :half], out_grad[:, half:]).astype(BF16)

    reps = partial.shape[0]
    stride = loops * OWN_ROWS
    start = OWN_ROWS * loop_index
    rows = jnp.concatenate(
        [pooled_rows[pl.ds(stride * rep + start, FOLD), :] for rep in range(reps)]
        + [pooled_rows[pl.ds(stride * rep + start + FOLD, 1), :] for rep in range(reps)],
        axis=0,
    ).astype(BF16)
    padded = jnp.concatenate([out_half, jnp.zeros((images, FOLD_AT - half), BF16)], axis=1)
    sums = dot(rows, padded)
    partial[:, :, :FOLD_AT] = sums[: reps * FOLD].reshape(reps, FOLD, FOLD_AT).astype(BF16)
    width = half // FOLD
    folded[...] = jnp.zeros(folded.shape, F32)
    for n in range(FOLD):
        folded[pl.ds(n, reps, FOLD), :width] = sums[reps * FOLD :, n * width : (n + 1) * width]
    partial[:, :, FOLD_AT:] = folded[...].reshape(reps, FOLD, MESSAGE - FOLD_AT).astype(BF16)

    pair_rows[:images] = jnp.transpose(pair_grad.astype(F32))
    pair_rows[images:] = jnp.zeros((pair_rows.shape[0] - images, images), F32)
    own = dot(pair_rows[pl.ds(own_rows * loop_index, 8), :].astype(BF16), embedded)
    txt_grad[...] = jnp.where(first, own[:own_rows, :half], own[:own_rows, half:])


def sum_kernel(blocks, text_sums, out, text_out):
    text_out[...] = text_sums[...]
    total = jnp.sum(blocks[...].astype(F32), axis=0)
    half = out.shape[1]
    width = half // FOLD
    out[:FOLD] = total[:, :half]
    out[FOLD:] = jnp.concatenate(
        [total[n : n + 1, FOLD_AT : FOLD_AT + width] for n in range(FOLD)], axis=1
    )


def local(reps, members, patches, positions, counts, probe, w_keyval, w_out, texts):
    vmem = pl.BlockSpec(memory_space=pltpu.VMEM)
    hbm = pl.BlockSpec(memory_space=pltpu.HBM)
    message = pl.pallas_call(
        pool_kernel,
        name="pool",
        out_shape=pltpu.VMEM((members, IMAGES + texts.shape[0] // 2, WIDTH), BF16),
        in_specs=[hbm] * 7,
        out_specs=vmem,
        scratch_shapes=[
            pltpu.SMEM((IMAGES,), jnp.int32),
            pltpu.VMEM(positions.shape, jnp.int32),
            pltpu.VMEM(probe.shape, BF16),
            pltpu.VMEM((2 * POSITIONS, 2 * POSITIONS), F32),
            pltpu.VMEM(texts.shape, BF16),
            pltpu.VMEM((IMAGES * SLOTS, WIDTH), BF16),
            pltpu.VMEM((WIDTH, WIDTH), BF16),
            pltpu.VMEM((WIDTH, WIDTH), BF16),
            pltpu.SemaphoreType.DMA((5,)),
            pltpu.SemaphoreType.DMA((IMAGES,)),
            pltpu.SemaphoreType.DMA,
            pltpu.SemaphoreType.DMA,
        ],
        compiler_params=pltpu.CompilerParams(vmem_limit_bytes=60 * 1024 * 1024),
    )(counts, positions, probe, jnp.asarray(angle_table()), texts, patches, w_keyval)
    message, w_out = lax.optimization_barrier((message, w_out))
    gathered = lax.all_to_all(message, ("loop", "seq"), split_axis=0, concat_axis=0, tiled=True)
    images = IMAGES * members
    txt_grad, partial = pl.pallas_call(
        pair_kernel,
        name="pairs",
        out_shape=(
            pltpu.VMEM(texts.shape, F32),
            pltpu.VMEM((reps, FOLD, MESSAGE), BF16),
        ),
        in_specs=[vmem, vmem],
        out_specs=(vmem, vmem),
        scratch_shapes=[
            pltpu.VMEM((images + 8, images), F32),
            pltpu.VMEM((WIDTH + 16, images), F32),
            pltpu.VMEM((reps * FOLD, MESSAGE - FOLD_AT), F32),
        ],
        compiler_params=pltpu.CompilerParams(vmem_limit_bytes=24 * 1024 * 1024),
    )(gathered, w_out)
    blocks = lax.all_to_all(partial, "rep", split_axis=0, concat_axis=0, tiled=True)
    wo_grad, txt_grad = pl.pallas_call(
        sum_kernel,
        name="sums",
        out_shape=(
            jax.ShapeDtypeStruct((OWN_ROWS, WIDTH // 2), F32),
            jax.ShapeDtypeStruct(texts.shape, F32),
        ),
        in_specs=[vmem, vmem],
        out_specs=(vmem, vmem),
        compiler_params=pltpu.CompilerParams(vmem_limit_bytes=16 * 1024 * 1024),
    )(blocks, txt_grad)
    return (txt_grad, wo_grad)


def solution(mesh):
    reps = mesh.shape["rep"]
    members = mesh.shape["loop"] * mesh.shape["seq"]
    return jax.shard_map(
        functools.partial(local, reps, members),
        mesh=mesh,
        in_specs=(
            P(("rep", "loop", "seq"), None, None),
            P(None, ("rep", "loop", "seq"), None),
            P(("rep", "loop", "seq")),
            P(),
            P(),
            P(),
            P(("rep", "loop"), "seq"),
        ),
        out_specs=(P(("rep", "loop"), "seq"), P(("rep", "loop"), "seq")),
        check_vma=False,
    )
```

```python
import functools

import jax
import jax.numpy as jnp
import numpy as np
from jax import lax
from jax.experimental import pallas as pl
from jax.experimental.pallas import tpu as pltpu
from jax.sharding import PartitionSpec as P

WIDTH = 1152
HEADS = 16
HEAD_DIM = 72
HALF = HEAD_DIM // 2
QUARTER = HEAD_DIM // 4
SLOTS = 256
IMAGES = 2
POSITIONS = 128

MASK_FILL = -1e30
LOGIT_SCALE = 10.0
LOGIT_BIAS = -2.0

GROUP = 40
OWN_ROWS = 9
FOLD = 8
FOLD_AT = 640
Z_ORDER = (4, 5, 6, 7, 3, 2, 1, 0)
MESSAGE = 768

BF16 = jnp.bfloat16
F32 = jnp.float32


def angle_table():
    freqs = 10000.0 ** (-np.arange(QUARTER) / QUARTER)
    angles = np.arange(POSITIONS)[:, None] * freqs[None, :]
    table = np.zeros((2 * POSITIONS, 2 * POSITIONS), np.float32)
    for kind, value in enumerate((np.cos(angles), np.sin(angles))):
        high = value.astype(BF16).astype(np.float64)
        for part, entry in enumerate((high, value - high)):
            start = (2 * part + kind) * GROUP
            table[:POSITIONS, start : start + QUARTER] = entry
            table[POSITIONS:, start + QUARTER : start + HALF] = entry
    return table


def dot(left, right, left_axis=1, right_axis=0):
    return lax.dot_general(
        left, right, (((left_axis,), (right_axis,)), ((), ())), preferred_element_type=F32
    )


def split(value):
    high = value.astype(BF16)
    return high, (value - high.astype(F32)).astype(BF16)


def pool_kernel(
    counts_hbm, positions_hbm, probe_hbm, table_hbm, texts_hbm, patches_hbm, weights_hbm, out,
    counts, positions, probe, table, texts, patches, w_key, w_val,
    small_sem, patch_sem, key_sem, val_sem,
):
    small = [
        pltpu.make_async_copy(source, target, small_sem.at[n])
        for n, (source, target) in enumerate(
            (
                (positions_hbm, positions),
                (table_hbm, table),
                (probe_hbm, probe),
                (texts_hbm, texts),
                (counts_hbm, counts),
            )
        )
    ]
    copies = [
        pltpu.make_async_copy(
            patches_hbm.at[image],
            patches.at[pl.ds(image * SLOTS, SLOTS)],
            patch_sem.at[image],
        )
        for image in range(IMAGES)
    ]
    copies.append(
        pltpu.make_async_copy(weights_hbm.at[:, pl.ds(0, WIDTH)], w_key, key_sem)
    )
    val_copy = pltpu.make_async_copy(weights_hbm.at[:, pl.ds(WIDTH, WIDTH)], w_val, val_sem)
    for copy in small + copies + [val_copy]:
        copy.start()
    for copy in small:
        copy.wait()

    pos = jnp.concatenate([positions[0], positions[1], jnp.zeros((4, SLOTS), jnp.int32)], axis=0)
    pos_t = jnp.transpose(pos.astype(F32))
    lane = lax.broadcasted_iota(jnp.int32, (SLOTS, POSITIONS), 1).astype(F32)
    hot = []
    for image in range(IMAGES):
        row = (pos_t[:, image : image + 1] == lane).astype(F32)
        col = (pos_t[:, 2 + image : 3 + image] == lane).astype(F32)
        hot.append(jnp.concatenate([row, col], axis=1))
    hot = jnp.concatenate(hot, axis=0).astype(BF16)
    cos_sin = dot(hot, table[...].astype(BF16)).astype(BF16)

    entry = lax.broadcasted_iota(jnp.int32, (8, WIDTH), 1) % HEAD_DIM
    within = entry % HALF
    own = jnp.broadcast_to(probe[...].astype(F32).reshape(1, WIDTH), (8, WIDTH))
    after = pltpu.roll(own, WIDTH - QUARTER, 1)
    before = pltpu.roll(own, QUARTER, 1)
    partner = jnp.where(within < QUARTER, after, -before)
    key = (entry // HALF) * QUARTER + within % QUARTER
    match = lax.broadcasted_iota(jnp.int32, (GROUP, WIDTH), 0) == key[:1]
    spread_cos = jnp.where(match, own[:1], 0.0)
    spread_sin = jnp.where(match, partner[:1], 0.0)
    spread = jnp.concatenate(
        [spread_cos, spread_sin, spread_cos, spread_sin,
         jnp.zeros((2 * POSITIONS - 4 * GROUP, WIDTH), F32)],
        axis=0,
    ).astype(BF16)

    head = lax.broadcasted_iota(jnp.int32, (HEADS, WIDTH), 0) * HEAD_DIM
    column = lax.broadcasted_iota(jnp.int32, (HEADS, WIDTH), 1)
    in_head = (column >= head) & (column < head + HEAD_DIM)

    head_row = lax.broadcasted_iota(jnp.int32, (WIDTH, HEADS), 0)
    head_lane = lax.broadcasted_iota(jnp.int32, (WIDTH, HEADS), 1) * HEAD_DIM
    head_cols = (head_row >= head_lane) & (head_row < head_lane + HEAD_DIM)
    head_cols = head_cols.astype(F32).astype(BF16)

    for copy in copies:
        copy.wait()
    keys = dot(patches[...], w_key[...])
    high, low = split(keys * dot(cos_sin, spread))
    scores = jnp.transpose(dot(high, head_cols) + dot(low, head_cols)) * HEAD_DIM ** (-0.5)

    slot = lax.broadcasted_iota(jnp.int32, (HEADS, SLOTS), 1)
    sums, totals = [], []
    for image in range(IMAGES):
        live = slot < counts[image]
        part = jnp.where(live, scores[:, image * SLOTS : (image + 1) * SLOTS], MASK_FILL)
        top = jnp.max(part, axis=1, keepdims=True)
        raised = jnp.where(live, jnp.exp(part - top), 0.0)
        totals.append(jnp.sum(raised, axis=1, keepdims=True))
        sums.append(dot(raised.astype(BF16), patches[pl.ds(image * SLOTS, SLOTS)]))
    high, low = split(jnp.concatenate(sums, axis=0))
    val_copy.wait()
    acc = dot(jnp.concatenate([high, low], axis=0), w_val[...])
    acc = acc[: IMAGES * HEADS] + acc[IMAGES * HEADS :]
    pooled = [
        jnp.sum(
            jnp.where(in_head, acc[image * HEADS : (image + 1) * HEADS] / totals[image], 0.0),
            axis=0,
            keepdims=True,
        )
        for image in range(IMAGES)
    ]
    text = texts[...].astype(F32)
    pairs = [
        jnp.concatenate([text[n : n + 1], text[n + 1 : n + 2]], axis=1)
        for n in range(0, texts.shape[0], 2)
    ]
    message = jnp.concatenate(pooled + pairs, axis=0).astype(BF16)
    for peer in range(out.shape[0]):
        out[peer] = message


def pair_kernel(gathered, w_out, txt_grad, partial, pair_rows, pooled_rows, folded):
    members = gathered.shape[0]
    groups = lax.axis_size("yh")
    group = lax.axis_index("yh")
    images = IMAGES * members
    loops = members // (2 * groups)
    own_rows = images // (loops * groups)
    half = WIDTH // 2
    loop_index = lax.axis_index("loop")
    first = lax.axis_index("seq") == 0

    height = gathered.shape[1]
    block = gathered[...].astype(F32).reshape(members * height, WIDTH).astype(BF16)
    row = lax.broadcasted_iota(jnp.int32, (images, members * height), 0)
    source = lax.broadcasted_iota(jnp.int32, (images, members * height), 1)
    pick_image = source == (members - 1 - row // IMAGES) * height + row % IMAGES
    text_source = (members - 1 - (row // own_rows) * 2) * height + IMAGES + (row % own_rows) // 2
    pick = [pick_image, source == text_source, source == text_source - height]
    pick = jnp.concatenate([one.astype(F32) for one in pick], axis=0).astype(BF16)
    compact = dot(pick, block)
    pooled_f32 = compact[:images]
    pooled = pooled_f32.astype(BF16)
    even = lax.broadcasted_iota(jnp.int32, (images, half), 0) % 2 == 0
    halves = [
        jnp.where(even, part[:, :half], part[:, half:])
        for part in (compact[images : 2 * images], compact[2 * images :])
    ]
    texts = jnp.concatenate(halves, axis=1).astype(BF16)
    pooled_rows[:WIDTH] = jnp.transpose(pooled_f32)
    pooled_rows[WIDTH:] = jnp.zeros((pooled_rows.shape[0] - WIDTH, images), F32)

    projected = dot(pooled, w_out[...])
    length = jnp.sqrt(jnp.sum(projected * projected, axis=1, keepdims=True) + 1e-06)
    unit = projected / length
    embedded = unit.astype(BF16)
    logit = LOGIT_SCALE * dot(embedded, texts, 1, 1) + LOGIT_BIAS
    same = lax.broadcasted_iota(jnp.int32, (images, images), 0) == lax.broadcasted_iota(
        jnp.int32, (images, images), 1
    )
    labels = jnp.where(same, 1.0, -1.0)
    block_size = images // groups
    together = lax.broadcasted_iota(jnp.int32, (images, images), 0) // block_size == (
        lax.broadcasted_iota(jnp.int32, (images, images), 1) // block_size
    )
    pair_grad = LOGIT_SCALE * (-labels * jax.nn.sigmoid(-labels * logit))
    pair_grad = jnp.where(together, pair_grad, 0.0).astype(BF16)
    image_grad = dot(pair_grad, texts)
    inner = jnp.sum(unit * image_grad, axis=1, keepdims=True)
    out_grad = ((image_grad - unit * inner) / length).astype(F32)
    out_half = jnp.where(first, out_grad[:, :half], out_grad[:, half:]).astype(BF16)

    reps = partial.shape[0]
    stride = loops * OWN_ROWS
    start = stride * reps * group + OWN_ROWS * loop_index
    rows = jnp.concatenate(
        [pooled_rows[pl.ds(stride * rep + start, FOLD), :] for rep in Z_ORDER]
        + [pooled_rows[pl.ds(stride * rep + start + FOLD, 1), :] for rep in Z_ORDER],
        axis=0,
    ).astype(BF16)
    padded = jnp.concatenate([out_half, jnp.zeros((images, FOLD_AT - half), BF16)], axis=1)
    sums = dot(rows, padded)
    partial[:, :, :FOLD_AT] = sums[: reps * FOLD].reshape(reps, FOLD, FOLD_AT).astype(BF16)
    width = half // FOLD
    folded[...] = jnp.zeros(folded.shape, F32)
    for n in range(FOLD):
        folded[pl.ds(n, reps, FOLD), :width] = sums[reps * FOLD :, n * width : (n + 1) * width]
    partial[:, :, FOLD_AT:] = folded[...].reshape(reps, FOLD, MESSAGE - FOLD_AT).astype(BF16)

    pair_rows[:images] = jnp.transpose(pair_grad.astype(F32))
    pair_rows[images:] = jnp.zeros((pair_rows.shape[0] - images, images), F32)
    own = dot(pair_rows[pl.ds(block_size * group + own_rows * loop_index, 8), :].astype(BF16), embedded)
    txt_grad[...] = jnp.where(first, own[:own_rows, :half], own[:own_rows, half:])


def sum_kernel(blocks, text_sums, out, text_out):
    text_out[...] = text_sums[...]
    total = jnp.sum(blocks[...].astype(F32), axis=0)
    half = out.shape[1]
    width = half // FOLD
    out[:FOLD] = total[:, :half]
    out[FOLD:] = jnp.concatenate(
        [total[n : n + 1, FOLD_AT : FOLD_AT + width] for n in range(FOLD)], axis=1
    )


def local(reps, members, patches, positions, counts, probe, w_keyval, w_out, texts):
    vmem = pl.BlockSpec(memory_space=pltpu.VMEM)
    hbm = pl.BlockSpec(memory_space=pltpu.HBM)
    message = pl.pallas_call(
        pool_kernel,
        name="pool",
        out_shape=pltpu.VMEM((members, IMAGES + texts.shape[0] // 2, WIDTH), BF16),
        in_specs=[hbm] * 7,
        out_specs=vmem,
        scratch_shapes=[
            pltpu.SMEM((IMAGES,), jnp.int32),
            pltpu.VMEM(positions.shape, jnp.int32),
            pltpu.VMEM(probe.shape, BF16),
            pltpu.VMEM((2 * POSITIONS, 2 * POSITIONS), F32),
            pltpu.VMEM(texts.shape, BF16),
            pltpu.VMEM((IMAGES * SLOTS, WIDTH), BF16),
            pltpu.VMEM((WIDTH, WIDTH), BF16),
            pltpu.VMEM((WIDTH, WIDTH), BF16),
            pltpu.SemaphoreType.DMA((5,)),
            pltpu.SemaphoreType.DMA((IMAGES,)),
            pltpu.SemaphoreType.DMA,
            pltpu.SemaphoreType.DMA,
        ],
        compiler_params=pltpu.CompilerParams(vmem_limit_bytes=60 * 1024 * 1024),
    )(counts, positions, probe, jnp.asarray(angle_table()), texts, patches, w_keyval)
    message, w_out = lax.optimization_barrier((message, w_out))
    gathered = lax.all_to_all(message, ("yh", "loop", "seq"), split_axis=0, concat_axis=0, tiled=True, axis_index_groups=[list(range(members))[::-1]])
    images = IMAGES * members
    txt_grad, partial = pl.pallas_call(
        pair_kernel,
        name="pairs",
        out_shape=(
            pltpu.VMEM(texts.shape, F32),
            pltpu.VMEM((reps, FOLD, MESSAGE), BF16),
        ),
        in_specs=[vmem, vmem],
        out_specs=(vmem, vmem),
        scratch_shapes=[
            pltpu.VMEM((images + 8, images), F32),
            pltpu.VMEM((WIDTH + 16, images), F32),
            pltpu.VMEM((reps * FOLD, MESSAGE - FOLD_AT), F32),
        ],
        compiler_params=pltpu.CompilerParams(vmem_limit_bytes=24 * 1024 * 1024),
    )(gathered, w_out)
    blocks = lax.all_to_all(partial, "z", split_axis=0, concat_axis=0, tiled=True, axis_index_groups=[list(Z_ORDER)])
    wo_grad, txt_grad = pl.pallas_call(
        sum_kernel,
        name="sums",
        out_shape=(
            jax.ShapeDtypeStruct((OWN_ROWS, WIDTH // 2), F32),
            jax.ShapeDtypeStruct(texts.shape, F32),
        ),
        in_specs=[vmem, vmem],
        out_specs=(vmem, vmem),
        compiler_params=pltpu.CompilerParams(vmem_limit_bytes=16 * 1024 * 1024),
    )(blocks, txt_grad)
    return (txt_grad, wo_grad)


def solution(mesh):
    split = (2, mesh.shape["rep"] // 2, mesh.shape["loop"], mesh.shape["seq"])
    mesh = jax.sharding.Mesh(mesh.devices.reshape(split), ("yh", "z", "loop", "seq"))
    reps = mesh.shape["z"]
    members = mesh.shape["yh"] * mesh.shape["loop"] * mesh.shape["seq"]
    every = ("yh", "z", "loop", "seq")
    return jax.shard_map(
        functools.partial(local, reps, members),
        mesh=mesh,
        in_specs=(
            P(every, None, None),
            P(None, every, None),
            P(every),
            P(),
            P(),
            P(),
            P(("yh", "z", "loop"), "seq"),
        ),
        out_specs=(P(("yh", "z", "loop"), "seq"), P(("yh", "z", "loop"), "seq")),
        check_vma=False,
    )
```

```python
import functools

import jax
import jax.numpy as jnp
import numpy as np
from jax import lax
from jax.experimental import pallas as pl
from jax.experimental.pallas import tpu as pltpu
from jax.sharding import PartitionSpec as P

WIDTH = 1152
HEADS = 16
HEAD_DIM = 72
HALF = HEAD_DIM // 2
QUARTER = HEAD_DIM // 4
SLOTS = 256
IMAGES = 2
POSITIONS = 128

MASK_FILL = -1e30
LOGIT_SCALE = 10.0
LOGIT_BIAS = -2.0

GROUP = 40
OWN_ROWS = 9
FOLD = 8
FOLD_AT = 640
MEMBER_ORDER = tuple(
    16 * y_hi + 4 * x + 2 * core + y_lo
    for x in (3, 2, 1, 0)
    for y_hi in (1, 0)
    for y_lo in (1, 0)
    for core in (1, 0)
)
REP_ORDER = (4, 5, 6, 7, 3, 2, 1, 0)
KEY_PARTS = ((0, 512), (512, 1152))
MESSAGE = 768

BF16 = jnp.bfloat16
F32 = jnp.float32


def angle_table():
    freqs = 10000.0 ** (-np.arange(QUARTER) / QUARTER)
    angles = np.arange(POSITIONS)[:, None] * freqs[None, :]
    table = np.zeros((2 * POSITIONS, 2 * POSITIONS), np.float32)
    for kind, value in enumerate((np.cos(angles), np.sin(angles))):
        high = value.astype(BF16).astype(np.float64)
        for part, entry in enumerate((high, value - high)):
            start = (2 * part + kind) * GROUP
            table[:POSITIONS, start : start + QUARTER] = entry
            table[POSITIONS:, start + QUARTER : start + HALF] = entry
    return table


def pick_table(members):
    height = 2 * IMAGES
    images = IMAGES * members
    at = {member: place * height for place, member in enumerate(MEMBER_ORDER)}
    table = np.zeros((3 * images, members * height), np.float32)
    for n in range(images):
        table[n, at[n // IMAGES] + n % IMAGES] = 1
        for half in range(2):
            place = at[n // 4 * 2 + half] + IMAGES + n % 4 // 2
            table[(1 + half) * images + n, place] = 1
    return table


def dot(left, right, left_axis=1, right_axis=0):
    return lax.dot_general(
        left, right, (((left_axis,), (right_axis,)), ((), ())), preferred_element_type=F32
    )


def split(value):
    high = value.astype(BF16)
    return high, (value - high.astype(F32)).astype(BF16)


def pool_kernel(
    counts_hbm, positions_hbm, probe_hbm, table_hbm, texts_hbm, patches_hbm, weights_hbm, w_out_hbm,
    out, w_out,
    counts, positions, probe, table, texts, turn, patches, w_key, w_val,
    small_sem, patch_sem, key_sem, val_sem, out_sem,
):
    small = [
        pltpu.make_async_copy(source, target, small_sem.at[n])
        for n, (source, target) in enumerate(
            (
                (positions_hbm, positions),
                (table_hbm, table),
                (probe_hbm, probe),
                (texts_hbm, texts),
                (counts_hbm, counts),
            )
        )
    ]
    copies = [
        pltpu.make_async_copy(
            patches_hbm.at[image],
            patches.at[pl.ds(image * SLOTS, SLOTS)],
            patch_sem.at[image],
        )
        for image in range(IMAGES)
    ]
    key_copies = [
        pltpu.make_async_copy(
            weights_hbm.at[:, pl.ds(lo, hi - lo)], w_key.at[:, pl.ds(lo, hi - lo)], key_sem.at[n]
        )
        for n, (lo, hi) in enumerate(KEY_PARTS)
    ]
    val_copy = pltpu.make_async_copy(weights_hbm.at[:, pl.ds(WIDTH, WIDTH)], w_val, val_sem)
    out_copy = pltpu.make_async_copy(w_out_hbm, w_out, out_sem)
    for copy in small + copies + key_copies + [val_copy, out_copy]:
        copy.start()
    for copy in small:
        copy.wait()

    pos = jnp.concatenate([positions[0], positions[1], jnp.zeros((4, SLOTS), jnp.int32)], axis=0)
    pos_t = jnp.transpose(pos.astype(F32))
    lane = lax.broadcasted_iota(jnp.int32, (SLOTS, POSITIONS), 1).astype(F32)
    hot = []
    for image in range(IMAGES):
        row = (pos_t[:, image : image + 1] == lane).astype(F32)
        col = (pos_t[:, 2 + image : 3 + image] == lane).astype(F32)
        hot.append(jnp.concatenate([row, col], axis=1))
    hot = jnp.concatenate(hot, axis=0).astype(BF16)
    cos_sin = dot(hot, table[...].astype(BF16)).astype(BF16)

    entry = lax.broadcasted_iota(jnp.int32, (8, WIDTH), 1) % HEAD_DIM
    within = entry % HALF
    own = jnp.broadcast_to(probe[...].astype(F32).reshape(1, WIDTH), (8, WIDTH))
    after = pltpu.roll(own, WIDTH - QUARTER, 1)
    before = pltpu.roll(own, QUARTER, 1)
    partner = jnp.where(within < QUARTER, after, -before)
    key = (entry // HALF) * QUARTER + within % QUARTER
    match = lax.broadcasted_iota(jnp.int32, (GROUP, WIDTH), 0) == key[:1]
    spread_cos = jnp.where(match, own[:1], 0.0)
    spread_sin = jnp.where(match, partner[:1], 0.0)
    spread = jnp.concatenate(
        [spread_cos, spread_sin, spread_cos, spread_sin,
         jnp.zeros((2 * POSITIONS - 4 * GROUP, WIDTH), F32)],
        axis=0,
    ).astype(BF16)

    head = lax.broadcasted_iota(jnp.int32, (HEADS, WIDTH), 0) * HEAD_DIM
    column = lax.broadcasted_iota(jnp.int32, (HEADS, WIDTH), 1)
    in_head = (column >= head) & (column < head + HEAD_DIM)

    head_row = lax.broadcasted_iota(jnp.int32, (WIDTH, HEADS), 0)
    head_lane = lax.broadcasted_iota(jnp.int32, (WIDTH, HEADS), 1) * HEAD_DIM
    head_cols = (head_row >= head_lane) & (head_row < head_lane + HEAD_DIM)
    head_cols = head_cols.astype(F32).astype(BF16)

    turn[...] = dot(cos_sin, spread)
    for copy in copies + key_copies[:1]:
        copy.wait()
    first_keys = dot(patches[...], w_key[:, : KEY_PARTS[0][1]])
    key_copies[1].wait()
    scores = jnp.zeros((IMAGES * SLOTS, HEADS), F32)
    for lo, hi in KEY_PARTS:
        keys = first_keys if lo == 0 else dot(patches[...], w_key[:, lo:hi])
        high, low = split(keys * turn[:, lo:hi])
        cols = head_cols[lo:hi]
        scores += dot(high, cols) + dot(low, cols)
    scores = jnp.transpose(scores) * HEAD_DIM ** (-0.5)

    slot = lax.broadcasted_iota(jnp.int32, (HEADS, SLOTS), 1)
    sums, totals = [], []
    for image in range(IMAGES):
        live = slot < counts[image]
        part = jnp.where(live, scores[:, image * SLOTS : (image + 1) * SLOTS], MASK_FILL)
        top = jnp.max(part, axis=1, keepdims=True)
        raised = jnp.where(live, jnp.exp(part - top), 0.0)
        totals.append(jnp.sum(raised, axis=1, keepdims=True))
        sums.append(dot(raised.astype(BF16), patches[pl.ds(image * SLOTS, SLOTS)]))
    high, low = split(jnp.concatenate(sums, axis=0))
    val_copy.wait()
    acc = dot(jnp.concatenate([high, low], axis=0), w_val[...])
    acc = acc[: IMAGES * HEADS] + acc[IMAGES * HEADS :]
    pooled = [
        jnp.sum(
            jnp.where(in_head, acc[image * HEADS : (image + 1) * HEADS] / totals[image], 0.0),
            axis=0,
            keepdims=True,
        )
        for image in range(IMAGES)
    ]
    text = texts[...].astype(F32)
    pairs = [
        jnp.concatenate([text[n : n + 1], text[n + 1 : n + 2]], axis=1)
        for n in range(0, texts.shape[0], 2)
    ]
    message = jnp.concatenate(pooled + pairs, axis=0).astype(BF16)
    for peer in range(out.shape[0]):
        out[peer] = message
    out_copy.wait()


def pair_kernel(gathered, w_out, pick_ref, txt_grad, partial, pair_rows, pooled_rows, folded):
    members = gathered.shape[0]
    groups = lax.axis_size("yh")
    group = lax.axis_index("yh")
    images = IMAGES * members
    loops = members // (2 * groups)
    own_rows = images // (loops * groups)
    half = WIDTH // 2
    loop_index = lax.axis_index("loop")
    first = lax.axis_index("seq") == 0

    height = gathered.shape[1]
    block = gathered[...].astype(F32).reshape(members * height, WIDTH).astype(BF16)
    pick = pick_ref[...].astype(BF16)
    compact = dot(pick, block)
    pooled_f32 = compact[:images]
    pooled = pooled_f32.astype(BF16)
    even = lax.broadcasted_iota(jnp.int32, (images, half), 0) % 2 == 0
    halves = [
        jnp.where(even, part[:, :half], part[:, half:])
        for part in (compact[images : 2 * images], compact[2 * images :])
    ]
    texts = jnp.concatenate(halves, axis=1).astype(BF16)
    pooled_rows[:WIDTH] = jnp.transpose(pooled_f32)
    pooled_rows[WIDTH:] = jnp.zeros((pooled_rows.shape[0] - WIDTH, images), F32)

    projected = dot(pooled, w_out[...])
    length = jnp.sqrt(jnp.sum(projected * projected, axis=1, keepdims=True) + 1e-06)
    unit = projected / length
    embedded = unit.astype(BF16)
    logit = LOGIT_SCALE * dot(embedded, texts, 1, 1) + LOGIT_BIAS
    same = lax.broadcasted_iota(jnp.int32, (images, images), 0) == lax.broadcasted_iota(
        jnp.int32, (images, images), 1
    )
    labels = jnp.where(same, 1.0, -1.0)
    block_size = images // groups
    together = lax.broadcasted_iota(jnp.int32, (images, images), 0) // block_size == (
        lax.broadcasted_iota(jnp.int32, (images, images), 1) // block_size
    )
    pair_grad = LOGIT_SCALE * (-labels * jax.nn.sigmoid(-labels * logit))
    pair_grad = jnp.where(together, pair_grad, 0.0).astype(BF16)
    image_grad = dot(pair_grad, texts)
    inner = jnp.sum(unit * image_grad, axis=1, keepdims=True)
    out_grad = ((image_grad - unit * inner) / length).astype(F32)
    out_half = jnp.where(first, out_grad[:, :half], out_grad[:, half:]).astype(BF16)

    reps = partial.shape[0]
    stride = loops * OWN_ROWS
    start = stride * reps * group + OWN_ROWS * loop_index
    rows = jnp.concatenate(
        [pooled_rows[pl.ds(stride * rep + start, FOLD), :] for rep in REP_ORDER]
        + [pooled_rows[pl.ds(stride * rep + start + FOLD, 1), :] for rep in REP_ORDER],
        axis=0,
    ).astype(BF16)
    padded = jnp.concatenate([out_half, jnp.zeros((images, FOLD_AT - half), BF16)], axis=1)
    sums = dot(rows, padded)
    partial[:, :, :FOLD_AT] = sums[: reps * FOLD].reshape(reps, FOLD, FOLD_AT).astype(BF16)
    width = half // FOLD
    folded[...] = jnp.zeros(folded.shape, F32)
    for n in range(FOLD):
        folded[pl.ds(n, reps, FOLD), :width] = sums[reps * FOLD :, n * width : (n + 1) * width]
    partial[:, :, FOLD_AT:] = folded[...].reshape(reps, FOLD, MESSAGE - FOLD_AT).astype(BF16)

    pair_rows[:images] = jnp.transpose(pair_grad.astype(F32))
    pair_rows[images:] = jnp.zeros((pair_rows.shape[0] - images, images), F32)
    own = dot(pair_rows[pl.ds(block_size * group + own_rows * loop_index, 8), :].astype(BF16), embedded)
    txt_grad[...] = jnp.where(first, own[:own_rows, :half], own[:own_rows, half:])


def sum_kernel(blocks, text_sums, out, text_out):
    text_out[...] = text_sums[...]
    total = jnp.sum(blocks[...].astype(F32), axis=0)
    half = out.shape[1]
    width = half // FOLD
    out[:FOLD] = total[:, :half]
    out[FOLD:] = jnp.concatenate(
        [total[n : n + 1, FOLD_AT : FOLD_AT + width] for n in range(FOLD)], axis=1
    )


def exchange(value, axis, order):
    return lax.all_to_all(
        value, axis, split_axis=0, concat_axis=0, tiled=True, axis_index_groups=[list(order)]
    )


def local(reps, members, patches, positions, counts, probe, w_keyval, w_out, texts):
    vmem = pl.BlockSpec(memory_space=pltpu.VMEM)
    hbm = pl.BlockSpec(memory_space=pltpu.HBM)
    message, w_out = pl.pallas_call(
        pool_kernel,
        name="pool",
        out_shape=(
            pltpu.VMEM((members, IMAGES + texts.shape[0] // 2, WIDTH), BF16),
            pltpu.VMEM(w_out.shape, BF16),
        ),
        in_specs=[hbm] * 8,
        out_specs=(vmem, vmem),
        scratch_shapes=[
            pltpu.SMEM((IMAGES,), jnp.int32),
            pltpu.VMEM(positions.shape, jnp.int32),
            pltpu.VMEM(probe.shape, BF16),
            pltpu.VMEM((2 * POSITIONS, 2 * POSITIONS), F32),
            pltpu.VMEM(texts.shape, BF16),
            pltpu.VMEM((IMAGES * SLOTS, WIDTH), F32),
            pltpu.VMEM((IMAGES * SLOTS, WIDTH), BF16),
            pltpu.VMEM((WIDTH, WIDTH), BF16),
            pltpu.VMEM((WIDTH, WIDTH), BF16),
            pltpu.SemaphoreType.DMA((5,)),
            pltpu.SemaphoreType.DMA((IMAGES,)),
            pltpu.SemaphoreType.DMA((len(KEY_PARTS),)),
            pltpu.SemaphoreType.DMA,
            pltpu.SemaphoreType.DMA,
        ],
        compiler_params=pltpu.CompilerParams(vmem_limit_bytes=60 * 1024 * 1024),
    )(counts, positions, probe, jnp.asarray(angle_table()), texts, patches, w_keyval, w_out)
    gathered = exchange(message, ("yh", "loop", "seq"), MEMBER_ORDER)
    images = IMAGES * members
    txt_grad, partial = pl.pallas_call(
        pair_kernel,
        name="pairs",
        out_shape=(
            pltpu.VMEM(texts.shape, F32),
            pltpu.VMEM((reps, FOLD, MESSAGE), BF16),
        ),
        in_specs=[vmem, vmem, vmem],
        out_specs=(vmem, vmem),
        scratch_shapes=[
            pltpu.VMEM((images + 8, images), F32),
            pltpu.VMEM((WIDTH + 16, images), F32),
            pltpu.VMEM((reps * FOLD, MESSAGE - FOLD_AT), F32),
        ],
        compiler_params=pltpu.CompilerParams(vmem_limit_bytes=24 * 1024 * 1024),
    )(gathered, w_out, jnp.asarray(pick_table(members)))
    blocks = exchange(partial, "z", REP_ORDER)
    wo_grad, txt_grad = pl.pallas_call(
        sum_kernel,
        name="sums",
        out_shape=(
            jax.ShapeDtypeStruct((OWN_ROWS, WIDTH // 2), F32),
            jax.ShapeDtypeStruct(texts.shape, F32),
        ),
        in_specs=[vmem, vmem],
        out_specs=(vmem, vmem),
        compiler_params=pltpu.CompilerParams(vmem_limit_bytes=16 * 1024 * 1024),
    )(blocks, txt_grad)
    return (txt_grad, wo_grad)


def solution(mesh):
    split = (2, mesh.shape["rep"] // 2, mesh.shape["loop"], mesh.shape["seq"])
    mesh = jax.sharding.Mesh(mesh.devices.reshape(split), ("yh", "z", "loop", "seq"))
    reps = mesh.shape["z"]
    members = mesh.shape["yh"] * mesh.shape["loop"] * mesh.shape["seq"]
    every = ("yh", "z", "loop", "seq")
    return jax.shard_map(
        functools.partial(local, reps, members),
        mesh=mesh,
        in_specs=(
            P(every, None, None),
            P(None, every, None),
            P(every),
            P(),
            P(),
            P(),
            P(("yh", "z", "loop"), "seq"),
        ),
        out_specs=(P(("yh", "z", "loop"), "seq"), P(("yh", "z", "loop"), "seq")),
        check_vma=False,
    )
```

```python
import functools

import jax
import jax.numpy as jnp
import numpy as np
from jax import lax
from jax.experimental import pallas as pl
from jax.experimental.pallas import tpu as pltpu
from jax.sharding import PartitionSpec as P

WIDTH = 1152
HEADS = 16
HEAD_DIM = 72
HALF = HEAD_DIM // 2
QUARTER = HEAD_DIM // 4
SLOTS = 256
IMAGES = 2
POSITIONS = 128

MASK_FILL = -1e30
LOGIT_SCALE = 10.0
LOGIT_BIAS = -2.0

GROUP = 40
OWN_ROWS = 9
FOLD = 8
FOLD_AT = 640
MEMBER_ORDER = tuple(
    16 * y_hi + 4 * x + 2 * core + y_lo
    for x in (2, 3, 1, 0)
    for y_hi in (1, 0)
    for y_lo in (1, 0)
    for core in (1, 0)
)
REP_ORDER = (4, 5, 6, 7, 3, 2, 1, 0)
KEY_PARTS = ((0, 512), (512, 1152))
MESSAGE = 768

BF16 = jnp.bfloat16
F32 = jnp.float32


def angle_table():
    freqs = 10000.0 ** (-np.arange(QUARTER) / QUARTER)
    angles = np.arange(POSITIONS)[:, None] * freqs[None, :]
    table = np.zeros((2 * POSITIONS, 2 * POSITIONS), np.float32)
    for kind, value in enumerate((np.cos(angles), np.sin(angles))):
        high = value.astype(BF16).astype(np.float64)
        for part, entry in enumerate((high, value - high)):
            start = (2 * part + kind) * GROUP
            table[:POSITIONS, start : start + QUARTER] = entry
            table[POSITIONS:, start + QUARTER : start + HALF] = entry
    return table


def pick_table(members):
    height = 2 * IMAGES
    images = IMAGES * members
    at = {member: place * height for place, member in enumerate(MEMBER_ORDER)}
    table = np.zeros((3 * images, members * height), np.float32)
    for n in range(images):
        table[n, at[n // IMAGES] + n % IMAGES] = 1
        for half in range(2):
            place = at[n // 4 * 2 + half] + IMAGES + n % 4 // 2
            table[(1 + half) * images + n, place] = 1
    return table


def dot(left, right, left_axis=1, right_axis=0):
    return lax.dot_general(
        left, right, (((left_axis,), (right_axis,)), ((), ())), preferred_element_type=F32
    )


def split(value):
    high = value.astype(BF16)
    return high, (value - high.astype(F32)).astype(BF16)


def pool_kernel(
    counts_hbm, positions_hbm, probe_hbm, table_hbm, texts_hbm, patches_hbm, weights_hbm, w_out_hbm,
    out, w_out,
    counts, positions, probe, table, texts, turn, patches, w_key, w_val,
    small_sem, patch_sem, key_sem, val_sem, out_sem,
):
    small = [
        pltpu.make_async_copy(source, target, small_sem.at[n])
        for n, (source, target) in enumerate(
            (
                (positions_hbm, positions),
                (table_hbm, table),
                (probe_hbm, probe),
                (texts_hbm, texts),
                (counts_hbm, counts),
            )
        )
    ]
    copies = [
        pltpu.make_async_copy(
            patches_hbm.at[image],
            patches.at[pl.ds(image * SLOTS, SLOTS)],
            patch_sem.at[image],
        )
        for image in range(IMAGES)
    ]
    key_copies = [
        pltpu.make_async_copy(
            weights_hbm.at[:, pl.ds(lo, hi - lo)], w_key.at[:, pl.ds(lo, hi - lo)], key_sem.at[n]
        )
        for n, (lo, hi) in enumerate(KEY_PARTS)
    ]
    val_copy = pltpu.make_async_copy(weights_hbm.at[:, pl.ds(WIDTH, WIDTH)], w_val, val_sem)
    out_copy = pltpu.make_async_copy(w_out_hbm, w_out, out_sem)
    for copy in small + copies + key_copies + [val_copy, out_copy]:
        copy.start()
    for copy in small:
        copy.wait()

    pos = jnp.concatenate([positions[0], positions[1], jnp.zeros((4, SLOTS), jnp.int32)], axis=0)
    pos_t = jnp.transpose(pos.astype(F32))
    lane = lax.broadcasted_iota(jnp.int32, (SLOTS, POSITIONS), 1).astype(F32)
    hot = []
    for image in range(IMAGES):
        row = (pos_t[:, image : image + 1] == lane).astype(F32)
        col = (pos_t[:, 2 + image : 3 + image] == lane).astype(F32)
        hot.append(jnp.concatenate([row, col], axis=1))
    hot = jnp.concatenate(hot, axis=0).astype(BF16)
    cos_sin = dot(hot, table[...].astype(BF16)).astype(BF16)

    entry = lax.broadcasted_iota(jnp.int32, (8, WIDTH), 1) % HEAD_DIM
    within = entry % HALF
    own = jnp.broadcast_to(probe[...].astype(F32).reshape(1, WIDTH), (8, WIDTH))
    after = pltpu.roll(own, WIDTH - QUARTER, 1)
    before = pltpu.roll(own, QUARTER, 1)
    partner = jnp.where(within < QUARTER, after, -before)
    key = (entry // HALF) * QUARTER + within % QUARTER
    match = lax.broadcasted_iota(jnp.int32, (GROUP, WIDTH), 0) == key[:1]
    spread_cos = jnp.where(match, own[:1], 0.0)
    spread_sin = jnp.where(match, partner[:1], 0.0)
    spread = jnp.concatenate(
        [spread_cos, spread_sin, spread_cos, spread_sin,
         jnp.zeros((2 * POSITIONS - 4 * GROUP, WIDTH), F32)],
        axis=0,
    ).astype(BF16)

    head = lax.broadcasted_iota(jnp.int32, (HEADS, WIDTH), 0) * HEAD_DIM
    column = lax.broadcasted_iota(jnp.int32, (HEADS, WIDTH), 1)
    in_head = (column >= head) & (column < head + HEAD_DIM)

    head_row = lax.broadcasted_iota(jnp.int32, (WIDTH, HEADS), 0)
    head_lane = lax.broadcasted_iota(jnp.int32, (WIDTH, HEADS), 1) * HEAD_DIM
    head_cols = (head_row >= head_lane) & (head_row < head_lane + HEAD_DIM)
    head_cols = head_cols.astype(F32).astype(BF16)

    turn[...] = dot(cos_sin, spread)
    for copy in copies + key_copies[:1]:
        copy.wait()
    first_keys = dot(patches[...], w_key[:, : KEY_PARTS[0][1]])
    key_copies[1].wait()
    scores = jnp.zeros((IMAGES * SLOTS, HEADS), F32)
    for lo, hi in KEY_PARTS:
        keys = first_keys if lo == 0 else dot(patches[...], w_key[:, lo:hi])
        high, low = split(keys * turn[:, lo:hi])
        cols = head_cols[lo:hi]
        scores += dot(high, cols) + dot(low, cols)
    scores = jnp.transpose(scores) * HEAD_DIM ** (-0.5)

    slot = lax.broadcasted_iota(jnp.int32, (HEADS, SLOTS), 1)
    sums, totals = [], []
    for image in range(IMAGES):
        live = slot < counts[image]
        part = jnp.where(live, scores[:, image * SLOTS : (image + 1) * SLOTS], MASK_FILL)
        top = jnp.max(part, axis=1, keepdims=True)
        raised = jnp.where(live, jnp.exp(part - top), 0.0)
        totals.append(jnp.sum(raised, axis=1, keepdims=True))
        sums.append(dot(raised.astype(BF16), patches[pl.ds(image * SLOTS, SLOTS)]))
    high, low = split(jnp.concatenate(sums, axis=0))
    val_copy.wait()
    acc = dot(jnp.concatenate([high, low], axis=0), w_val[...])
    acc = acc[: IMAGES * HEADS] + acc[IMAGES * HEADS :]
    pooled = [
        jnp.sum(
            jnp.where(in_head, acc[image * HEADS : (image + 1) * HEADS] / totals[image], 0.0),
            axis=0,
            keepdims=True,
        )
        for image in range(IMAGES)
    ]
    text = texts[...].astype(F32)
    pairs = [
        jnp.concatenate([text[n : n + 1], text[n + 1 : n + 2]], axis=1)
        for n in range(0, texts.shape[0], 2)
    ]
    message = jnp.concatenate(pooled + pairs, axis=0).astype(BF16)
    for peer in range(out.shape[0]):
        out[peer] = message
    out_copy.wait()


def pair_kernel(gathered, w_out, pick_ref, txt_grad, partial, pair_rows, pooled_rows, folded):
    members = gathered.shape[0]
    groups = lax.axis_size("yh")
    group = lax.axis_index("yh")
    images = IMAGES * members
    loops = members // (2 * groups)
    own_rows = images // (loops * groups)
    half = WIDTH // 2
    loop_index = lax.axis_index("loop")
    first = lax.axis_index("seq") == 0

    height = gathered.shape[1]
    block = gathered[...].astype(F32).reshape(members * height, WIDTH).astype(BF16)
    pick = pick_ref[...].astype(BF16)
    compact = dot(pick, block)
    pooled_f32 = compact[:images]
    pooled = pooled_f32.astype(BF16)
    even = lax.broadcasted_iota(jnp.int32, (images, half), 0) % 2 == 0
    halves = [
        jnp.where(even, part[:, :half], part[:, half:])
        for part in (compact[images : 2 * images], compact[2 * images :])
    ]
    texts = jnp.concatenate(halves, axis=1).astype(BF16)
    pooled_rows[:WIDTH] = jnp.transpose(pooled_f32)
    pooled_rows[WIDTH:] = jnp.zeros((pooled_rows.shape[0] - WIDTH, images), F32)

    projected = dot(pooled, w_out[...])
    length = jnp.sqrt(jnp.sum(projected * projected, axis=1, keepdims=True) + 1e-06)
    unit = projected / length
    embedded = unit.astype(BF16)
    logit = LOGIT_SCALE * dot(embedded, texts, 1, 1) + LOGIT_BIAS
    same = lax.broadcasted_iota(jnp.int32, (images, images), 0) == lax.broadcasted_iota(
        jnp.int32, (images, images), 1
    )
    labels = jnp.where(same, 1.0, -1.0)
    block_size = images // groups
    together = lax.broadcasted_iota(jnp.int32, (images, images), 0) // block_size == (
        lax.broadcasted_iota(jnp.int32, (images, images), 1) // block_size
    )
    pair_grad = LOGIT_SCALE * (-labels * jax.nn.sigmoid(-labels * logit))
    pair_grad = jnp.where(together, pair_grad, 0.0).astype(BF16)
    image_grad = dot(pair_grad, texts)
    inner = jnp.sum(unit * image_grad, axis=1, keepdims=True)
    out_grad = ((image_grad - unit * inner) / length).astype(F32)
    out_half = jnp.where(first, out_grad[:, :half], out_grad[:, half:]).astype(BF16)

    reps = partial.shape[0]
    stride = loops * OWN_ROWS
    start = stride * reps * group + OWN_ROWS * loop_index
    rows = jnp.concatenate(
        [pooled_rows[pl.ds(stride * rep + start, FOLD), :] for rep in REP_ORDER]
        + [pooled_rows[pl.ds(stride * rep + start + FOLD, 1), :] for rep in REP_ORDER],
        axis=0,
    ).astype(BF16)
    padded = jnp.concatenate([out_half, jnp.zeros((images, FOLD_AT - half), BF16)], axis=1)
    sums = dot(rows, padded)
    partial[:, :, :FOLD_AT] = sums[: reps * FOLD].reshape(reps, FOLD, FOLD_AT).astype(BF16)
    width = half // FOLD
    folded[...] = jnp.zeros(folded.shape, F32)
    for n in range(FOLD):
        folded[pl.ds(n, reps, FOLD), :width] = sums[reps * FOLD :, n * width : (n + 1) * width]
    partial[:, :, FOLD_AT:] = folded[...].reshape(reps, FOLD, MESSAGE - FOLD_AT).astype(BF16)

    pair_rows[:images] = jnp.transpose(pair_grad.astype(F32))
    pair_rows[images:] = jnp.zeros((pair_rows.shape[0] - images, images), F32)
    own = dot(pair_rows[pl.ds(block_size * group + own_rows * loop_index, 8), :].astype(BF16), embedded)
    txt_grad[...] = jnp.where(first, own[:own_rows, :half], own[:own_rows, half:])


def sum_kernel(blocks, text_sums, out, text_out):
    text_out[...] = text_sums[...]
    total = jnp.sum(blocks[...].astype(F32), axis=0)
    half = out.shape[1]
    width = half // FOLD
    out[:FOLD] = total[:, :half]
    out[FOLD:] = jnp.concatenate(
        [total[n : n + 1, FOLD_AT : FOLD_AT + width] for n in range(FOLD)], axis=1
    )


def exchange(value, axis, order):
    return lax.all_to_all(
        value, axis, split_axis=0, concat_axis=0, tiled=True, axis_index_groups=[list(order)]
    )


def local(reps, members, patches, positions, counts, probe, w_keyval, w_out, texts):
    vmem = pl.BlockSpec(memory_space=pltpu.VMEM)
    hbm = pl.BlockSpec(memory_space=pltpu.HBM)
    message, w_out = pl.pallas_call(
        pool_kernel,
        name="pool",
        out_shape=(
            pltpu.VMEM((members, IMAGES + texts.shape[0] // 2, WIDTH), BF16),
            pltpu.VMEM(w_out.shape, BF16),
        ),
        in_specs=[hbm] * 8,
        out_specs=(vmem, vmem),
        scratch_shapes=[
            pltpu.SMEM((IMAGES,), jnp.int32),
            pltpu.VMEM(positions.shape, jnp.int32),
            pltpu.VMEM(probe.shape, BF16),
            pltpu.VMEM((2 * POSITIONS, 2 * POSITIONS), F32),
            pltpu.VMEM(texts.shape, BF16),
            pltpu.VMEM((IMAGES * SLOTS, WIDTH), F32),
            pltpu.VMEM((IMAGES * SLOTS, WIDTH), BF16),
            pltpu.VMEM((WIDTH, WIDTH), BF16),
            pltpu.VMEM((WIDTH, WIDTH), BF16),
            pltpu.SemaphoreType.DMA((5,)),
            pltpu.SemaphoreType.DMA((IMAGES,)),
            pltpu.SemaphoreType.DMA((len(KEY_PARTS),)),
            pltpu.SemaphoreType.DMA,
            pltpu.SemaphoreType.DMA,
        ],
        compiler_params=pltpu.CompilerParams(vmem_limit_bytes=60 * 1024 * 1024),
    )(counts, positions, probe, jnp.asarray(angle_table()), texts, patches, w_keyval, w_out)
    gathered = exchange(message, ("yh", "loop", "seq"), MEMBER_ORDER)
    images = IMAGES * members
    txt_grad, partial = pl.pallas_call(
        pair_kernel,
        name="pairs",
        out_shape=(
            pltpu.VMEM(texts.shape, F32),
            pltpu.VMEM((reps, FOLD, MESSAGE), BF16),
        ),
        in_specs=[vmem, vmem, vmem],
        out_specs=(vmem, vmem),
        scratch_shapes=[
            pltpu.VMEM((images + 8, images), F32),
            pltpu.VMEM((WIDTH + 16, images), F32),
            pltpu.VMEM((reps * FOLD, MESSAGE - FOLD_AT), F32),
        ],
        compiler_params=pltpu.CompilerParams(vmem_limit_bytes=24 * 1024 * 1024),
    )(gathered, w_out, jnp.asarray(pick_table(members)))
    blocks = exchange(partial, "z", REP_ORDER)
    wo_grad, txt_grad = pl.pallas_call(
        sum_kernel,
        name="sums",
        out_shape=(
            jax.ShapeDtypeStruct((OWN_ROWS, WIDTH // 2), F32),
            jax.ShapeDtypeStruct(texts.shape, F32),
        ),
        in_specs=[vmem, vmem],
        out_specs=(vmem, vmem),
        compiler_params=pltpu.CompilerParams(vmem_limit_bytes=16 * 1024 * 1024),
    )(blocks, txt_grad)
    return (txt_grad, wo_grad)


def solution(mesh):
    split = (2, mesh.shape["rep"] // 2, mesh.shape["loop"], mesh.shape["seq"])
    mesh = jax.sharding.Mesh(mesh.devices.reshape(split), ("yh", "z", "loop", "seq"))
    reps = mesh.shape["z"]
    members = mesh.shape["yh"] * mesh.shape["loop"] * mesh.shape["seq"]
    every = ("yh", "z", "loop", "seq")
    return jax.shard_map(
        functools.partial(local, reps, members),
        mesh=mesh,
        in_specs=(
            P(every, None, None),
            P(None, every, None),
            P(every),
            P(),
            P(),
            P(),
            P(("yh", "z", "loop"), "seq"),
        ),
        out_specs=(P(("yh", "z", "loop"), "seq"), P(("yh", "z", "loop"), "seq")),
        check_vma=False,
    )
```

```python
import functools

import jax
import jax.numpy as jnp
import numpy as np
from jax import lax
from jax.experimental import pallas as pl
from jax.experimental.pallas import tpu as pltpu
from jax.sharding import PartitionSpec as P

WIDTH = 1152
HEADS = 16
HEAD_DIM = 72
HALF = HEAD_DIM // 2
QUARTER = HEAD_DIM // 4
SLOTS = 256
IMAGES = 2
POSITIONS = 128

MASK_FILL = -1e30
LOGIT_SCALE = 10.0
LOGIT_BIAS = -2.0

GROUP = 40
OWN_ROWS = 9
FOLD = 8
FOLD_AT = 640
MEMBER_ORDER = tuple(
    16 * y_hi + 4 * x + 2 * core + y_lo
    for x in (2, 1, 3, 0)
    for y_hi in (1, 0)
    for y_lo in (1, 0)
    for core in (1, 0)
)
REP_ORDER = (4, 5, 6, 7, 3, 2, 1, 0)
KEY_PARTS = ((0, 512), (512, 1152))
MESSAGE = 768

BF16 = jnp.bfloat16
F32 = jnp.float32


def angle_table():
    freqs = 10000.0 ** (-np.arange(QUARTER) / QUARTER)
    angles = np.arange(POSITIONS)[:, None] * freqs[None, :]
    table = np.zeros((2 * POSITIONS, 2 * POSITIONS), np.float32)
    for kind, value in enumerate((np.cos(angles), np.sin(angles))):
        high = value.astype(BF16).astype(np.float64)
        for part, entry in enumerate((high, value - high)):
            start = (2 * part + kind) * GROUP
            table[:POSITIONS, start : start + QUARTER] = entry
            table[POSITIONS:, start + QUARTER : start + HALF] = entry
    return table


def pick_table(members):
    height = 2 * IMAGES
    images = IMAGES * members
    at = {member: place * height for place, member in enumerate(MEMBER_ORDER)}
    table = np.zeros((3 * images, members * height), np.float32)
    for n in range(images):
        table[n, at[n // IMAGES] + n % IMAGES] = 1
        for half in range(2):
            place = at[n // 4 * 2 + half] + IMAGES + n % 4 // 2
            table[(1 + half) * images + n, place] = 1
    return table


def dot(left, right, left_axis=1, right_axis=0):
    return lax.dot_general(
        left, right, (((left_axis,), (right_axis,)), ((), ())), preferred_element_type=F32
    )


def split(value):
    high = value.astype(BF16)
    return high, (value - high.astype(F32)).astype(BF16)


def pool_kernel(
    counts_hbm, positions_hbm, probe_hbm, table_hbm, texts_hbm, patches_hbm, weights_hbm, w_out_hbm,
    out, w_out,
    counts, positions, probe, table, texts, turn, patches, w_key, w_val,
    small_sem, patch_sem, key_sem, val_sem, out_sem,
):
    small = [
        pltpu.make_async_copy(source, target, small_sem.at[n])
        for n, (source, target) in enumerate(
            (
                (positions_hbm, positions),
                (table_hbm, table),
                (probe_hbm, probe),
                (texts_hbm, texts),
                (counts_hbm, counts),
            )
        )
    ]
    copies = [
        pltpu.make_async_copy(
            patches_hbm.at[image],
            patches.at[pl.ds(image * SLOTS, SLOTS)],
            patch_sem.at[image],
        )
        for image in range(IMAGES)
    ]
    key_copies = [
        pltpu.make_async_copy(
            weights_hbm.at[:, pl.ds(lo, hi - lo)], w_key.at[:, pl.ds(lo, hi - lo)], key_sem.at[n]
        )
        for n, (lo, hi) in enumerate(KEY_PARTS)
    ]
    val_copy = pltpu.make_async_copy(weights_hbm.at[:, pl.ds(WIDTH, WIDTH)], w_val, val_sem)
    out_copy = pltpu.make_async_copy(w_out_hbm, w_out, out_sem)
    for copy in small + copies + key_copies + [val_copy, out_copy]:
        copy.start()
    for copy in small:
        copy.wait()

    pos = jnp.concatenate([positions[0], positions[1], jnp.zeros((4, SLOTS), jnp.int32)], axis=0)
    pos_t = jnp.transpose(pos.astype(F32))
    lane = lax.broadcasted_iota(jnp.int32, (SLOTS, POSITIONS), 1).astype(F32)
    hot = []
    for image in range(IMAGES):
        row = (pos_t[:, image : image + 1] == lane).astype(F32)
        col = (pos_t[:, 2 + image : 3 + image] == lane).astype(F32)
        hot.append(jnp.concatenate([row, col], axis=1))
    hot = jnp.concatenate(hot, axis=0).astype(BF16)
    cos_sin = dot(hot, table[...].astype(BF16)).astype(BF16)

    entry = lax.broadcasted_iota(jnp.int32, (8, WIDTH), 1) % HEAD_DIM
    within = entry % HALF
    own = jnp.broadcast_to(probe[...].astype(F32).reshape(1, WIDTH), (8, WIDTH))
    after = pltpu.roll(own, WIDTH - QUARTER, 1)
    before = pltpu.roll(own, QUARTER, 1)
    partner = jnp.where(within < QUARTER, after, -before)
    key = (entry // HALF) * QUARTER + within % QUARTER
    match = lax.broadcasted_iota(jnp.int32, (GROUP, WIDTH), 0) == key[:1]
    spread_cos = jnp.where(match, own[:1], 0.0)
    spread_sin = jnp.where(match, partner[:1], 0.0)
    spread = jnp.concatenate(
        [spread_cos, spread_sin, spread_cos, spread_sin,
         jnp.zeros((2 * POSITIONS - 4 * GROUP, WIDTH), F32)],
        axis=0,
    ).astype(BF16)

    head = lax.broadcasted_iota(jnp.int32, (HEADS, WIDTH), 0) * HEAD_DIM
    column = lax.broadcasted_iota(jnp.int32, (HEADS, WIDTH), 1)
    in_head = (column >= head) & (column < head + HEAD_DIM)

    head_row = lax.broadcasted_iota(jnp.int32, (WIDTH, HEADS), 0)
    head_lane = lax.broadcasted_iota(jnp.int32, (WIDTH, HEADS), 1) * HEAD_DIM
    head_cols = (head_row >= head_lane) & (head_row < head_lane + HEAD_DIM)
    head_cols = head_cols.astype(F32).astype(BF16)

    turn[...] = dot(cos_sin, spread)
    for copy in copies + key_copies[:1]:
        copy.wait()
    first_keys = dot(patches[...], w_key[:, : KEY_PARTS[0][1]])
    key_copies[1].wait()
    scores = jnp.zeros((IMAGES * SLOTS, HEADS), F32)
    for lo, hi in KEY_PARTS:
        keys = first_keys if lo == 0 else dot(patches[...], w_key[:, lo:hi])
        high, low = split(keys * turn[:, lo:hi])
        cols = head_cols[lo:hi]
        scores += dot(high, cols) + dot(low, cols)
    scores = jnp.transpose(scores) * HEAD_DIM ** (-0.5)

    slot = lax.broadcasted_iota(jnp.int32, (HEADS, SLOTS), 1)
    sums, totals = [], []
    for image in range(IMAGES):
        live = slot < counts[image]
        part = jnp.where(live, scores[:, image * SLOTS : (image + 1) * SLOTS], MASK_FILL)
        top = jnp.max(part, axis=1, keepdims=True)
        raised = jnp.where(live, jnp.exp(part - top), 0.0)
        totals.append(jnp.sum(raised, axis=1, keepdims=True))
        sums.append(dot(raised.astype(BF16), patches[pl.ds(image * SLOTS, SLOTS)]))
    high, low = split(jnp.concatenate(sums, axis=0))
    val_copy.wait()
    acc = dot(jnp.concatenate([high, low], axis=0), w_val[...])
    acc = acc[: IMAGES * HEADS] + acc[IMAGES * HEADS :]
    pooled = [
        jnp.sum(
            jnp.where(in_head, acc[image * HEADS : (image + 1) * HEADS] / totals[image], 0.0),
            axis=0,
            keepdims=True,
        )
        for image in range(IMAGES)
    ]
    text = texts[...].astype(F32)
    pairs = [
        jnp.concatenate([text[n : n + 1], text[n + 1 : n + 2]], axis=1)
        for n in range(0, texts.shape[0], 2)
    ]
    message = jnp.concatenate(pooled + pairs, axis=0).astype(BF16)
    for peer in range(out.shape[0]):
        out[peer] = message
    out_copy.wait()


def pair_kernel(gathered, w_out, pick_ref, txt_grad, partial, pair_rows, pooled_rows, folded):
    members = gathered.shape[0]
    groups = lax.axis_size("yh")
    group = lax.axis_index("yh")
    images = IMAGES * members
    loops = members // (2 * groups)
    own_rows = images // (loops * groups)
    half = WIDTH // 2
    loop_index = lax.axis_index("loop")
    first = lax.axis_index("seq") == 0

    height = gathered.shape[1]
    block = gathered[...].astype(F32).reshape(members * height, WIDTH).astype(BF16)
    pick = pick_ref[...].astype(BF16)
    compact = dot(pick, block)
    pooled_f32 = compact[:images]
    pooled = pooled_f32.astype(BF16)
    even = lax.broadcasted_iota(jnp.int32, (images, half), 0) % 2 == 0
    halves = [
        jnp.where(even, part[:, :half], part[:, half:])
        for part in (compact[images : 2 * images], compact[2 * images :])
    ]
    texts = jnp.concatenate(halves, axis=1).astype(BF16)
    pooled_rows[:WIDTH] = jnp.transpose(pooled_f32)
    pooled_rows[WIDTH:] = jnp.zeros((pooled_rows.shape[0] - WIDTH, images), F32)

    projected = dot(pooled, w_out[...])
    length = jnp.sqrt(jnp.sum(projected * projected, axis=1, keepdims=True) + 1e-06)
    unit = projected / length
    embedded = unit.astype(BF16)
    logit = LOGIT_SCALE * dot(embedded, texts, 1, 1) + LOGIT_BIAS
    same = lax.broadcasted_iota(jnp.int32, (images, images), 0) == lax.broadcasted_iota(
        jnp.int32, (images, images), 1
    )
    labels = jnp.where(same, 1.0, -1.0)
    block_size = images // groups
    together = lax.broadcasted_iota(jnp.int32, (images, images), 0) // block_size == (
        lax.broadcasted_iota(jnp.int32, (images, images), 1) // block_size
    )
    pair_grad = LOGIT_SCALE * (-labels * jax.nn.sigmoid(-labels * logit))
    pair_grad = jnp.where(together, pair_grad, 0.0).astype(BF16)
    image_grad = dot(pair_grad, texts)
    inner = jnp.sum(unit * image_grad, axis=1, keepdims=True)
    out_grad = ((image_grad - unit * inner) / length).astype(F32)
    out_half = jnp.where(first, out_grad[:, :half], out_grad[:, half:]).astype(BF16)

    reps = partial.shape[0]
    stride = loops * OWN_ROWS
    start = stride * reps * group + OWN_ROWS * loop_index
    rows = jnp.concatenate(
        [pooled_rows[pl.ds(stride * rep + start, FOLD), :] for rep in REP_ORDER]
        + [pooled_rows[pl.ds(stride * rep + start + FOLD, 1), :] for rep in REP_ORDER],
        axis=0,
    ).astype(BF16)
    padded = jnp.concatenate([out_half, jnp.zeros((images, FOLD_AT - half), BF16)], axis=1)
    sums = dot(rows, padded)
    partial[:, :, :FOLD_AT] = sums[: reps * FOLD].reshape(reps, FOLD, FOLD_AT).astype(BF16)
    width = half // FOLD
    folded[...] = jnp.zeros(folded.shape, F32)
    for n in range(FOLD):
        folded[pl.ds(n, reps, FOLD), :width] = sums[reps * FOLD :, n * width : (n + 1) * width]
    partial[:, :, FOLD_AT:] = folded[...].reshape(reps, FOLD, MESSAGE - FOLD_AT).astype(BF16)

    pair_rows[:images] = jnp.transpose(pair_grad.astype(F32))
    pair_rows[images:] = jnp.zeros((pair_rows.shape[0] - images, images), F32)
    own = dot(pair_rows[pl.ds(block_size * group + own_rows * loop_index, 8), :].astype(BF16), embedded)
    txt_grad[...] = jnp.where(first, own[:own_rows, :half], own[:own_rows, half:])


def sum_kernel(blocks, text_sums, out, text_out):
    text_out[...] = text_sums[...]
    total = jnp.sum(blocks[...].astype(F32), axis=0)
    half = out.shape[1]
    width = half // FOLD
    out[:FOLD] = total[:, :half]
    out[FOLD:] = jnp.concatenate(
        [total[n : n + 1, FOLD_AT : FOLD_AT + width] for n in range(FOLD)], axis=1
    )


def exchange(value, axis, order):
    return lax.all_to_all(
        value, axis, split_axis=0, concat_axis=0, tiled=True, axis_index_groups=[list(order)]
    )


def local(reps, members, patches, positions, counts, probe, w_keyval, w_out, texts):
    vmem = pl.BlockSpec(memory_space=pltpu.VMEM)
    hbm = pl.BlockSpec(memory_space=pltpu.HBM)
    message, w_out = pl.pallas_call(
        pool_kernel,
        name="pool",
        out_shape=(
            pltpu.VMEM((members, IMAGES + texts.shape[0] // 2, WIDTH), BF16),
            pltpu.VMEM(w_out.shape, BF16),
        ),
        in_specs=[hbm] * 8,
        out_specs=(vmem, vmem),
        scratch_shapes=[
            pltpu.SMEM((IMAGES,), jnp.int32),
            pltpu.VMEM(positions.shape, jnp.int32),
            pltpu.VMEM(probe.shape, BF16),
            pltpu.VMEM((2 * POSITIONS, 2 * POSITIONS), F32),
            pltpu.VMEM(texts.shape, BF16),
            pltpu.VMEM((IMAGES * SLOTS, WIDTH), F32),
            pltpu.VMEM((IMAGES * SLOTS, WIDTH), BF16),
            pltpu.VMEM((WIDTH, WIDTH), BF16),
            pltpu.VMEM((WIDTH, WIDTH), BF16),
            pltpu.SemaphoreType.DMA((5,)),
            pltpu.SemaphoreType.DMA((IMAGES,)),
            pltpu.SemaphoreType.DMA((len(KEY_PARTS),)),
            pltpu.SemaphoreType.DMA,
            pltpu.SemaphoreType.DMA,
        ],
        compiler_params=pltpu.CompilerParams(vmem_limit_bytes=60 * 1024 * 1024),
    )(counts, positions, probe, jnp.asarray(angle_table()), texts, patches, w_keyval, w_out)
    gathered = exchange(message, ("yh", "loop", "seq"), MEMBER_ORDER)
    images = IMAGES * members
    txt_grad, partial = pl.pallas_call(
        pair_kernel,
        name="pairs",
        out_shape=(
            pltpu.VMEM(texts.shape, F32),
            pltpu.VMEM((reps, FOLD, MESSAGE), BF16),
        ),
        in_specs=[vmem, vmem, vmem],
        out_specs=(vmem, vmem),
        scratch_shapes=[
            pltpu.VMEM((images + 8, images), F32),
            pltpu.VMEM((WIDTH + 16, images), F32),
            pltpu.VMEM((reps * FOLD, MESSAGE - FOLD_AT), F32),
        ],
        compiler_params=pltpu.CompilerParams(vmem_limit_bytes=24 * 1024 * 1024),
    )(gathered, w_out, jnp.asarray(pick_table(members)))
    blocks = exchange(partial, "z", REP_ORDER)
    wo_grad, txt_grad = pl.pallas_call(
        sum_kernel,
        name="sums",
        out_shape=(
            jax.ShapeDtypeStruct((OWN_ROWS, WIDTH // 2), F32),
            jax.ShapeDtypeStruct(texts.shape, F32),
        ),
        in_specs=[vmem, vmem],
        out_specs=(vmem, vmem),
        compiler_params=pltpu.CompilerParams(vmem_limit_bytes=16 * 1024 * 1024),
    )(blocks, txt_grad)
    return (txt_grad, wo_grad)


def solution(mesh):
    split = (2, mesh.shape["rep"] // 2, mesh.shape["loop"], mesh.shape["seq"])
    mesh = jax.sharding.Mesh(mesh.devices.reshape(split), ("yh", "z", "loop", "seq"))
    reps = mesh.shape["z"]
    members = mesh.shape["yh"] * mesh.shape["loop"] * mesh.shape["seq"]
    every = ("yh", "z", "loop", "seq")
    return jax.shard_map(
        functools.partial(local, reps, members),
        mesh=mesh,
        in_specs=(
            P(every, None, None),
            P(None, every, None),
            P(every),
            P(),
            P(),
            P(),
            P(("yh", "z", "loop"), "seq"),
        ),
        out_specs=(P(("yh", "z", "loop"), "seq"), P(("yh", "z", "loop"), "seq")),
        check_vma=False,
    )
```
